32 devices in a mesh: batch: 8 (over z, x), tensor: 4 (over y, core).
Axes of the slice: x: 2, y: 2, z: 4, core: 2. Of those that a mesh axis runs over, the one named last changes fastest.
Arguments:
- tokens: bfloat16 [2048, 4096], P(('batch', 'tensor')), may hold values from -6 to 6
- norm_gain: float32 [4096], replicated, may hold values from 0.1 to 1.9
- w_query: bfloat16 [4096, 4096], P(None, 'tensor'), may hold values from -0.09375 to 0.09375
- w_key: bfloat16 [4096, 1024], P(None, 'tensor'), may hold values from -0.25 to 0.25
- w_value: bfloat16 [4096, 1024], P(None, 'tensor'), may hold values from -0.09375 to 0.09375
- w_out: bfloat16 [4096, 4096], P('tensor'), may hold values from -0.25 to 0.25
- prefix_keys: bfloat16 [4096, 1024], P('batch', 'tensor'), may hold values from -6 to 6
- prefix_values: bfloat16 [4096, 1024], P('batch', 'tensor'), may hold values from -6 to 6
- cache_keys: bfloat16 [36864, 1024], P('batch', 'tensor'), may hold values from -160 to 160
- cache_values: bfloat16 [36864, 1024], P('batch', 'tensor'), may hold values from -6 to 6
- cache_lengths: int32 [32], replicated, may hold values from 128 to 2048, as said below
- prefix_used: int32 [32], P('batch'), may hold values from 1024 to 4096
- parents: int32 [32, 64], P('batch'), may hold values from 0 to 62, as said below
- accepted_index: int32 [32, 8], P('batch'), may hold values from 0 to 63, as said below
Outputs:
- mixed_output: bfloat16 [2048, 4096], P(('batch', 'tensor'))
- accepted_keys: bfloat16 [32, 8, 1024], P('batch', None, 'tensor')
- accepted_values: bfloat16 [32, 8, 1024], P('batch', None, 'tensor')
The draws below stay inside these ranges and needn't reach their ends.
Inputs may be any that keep to these rules, and one draw needn't show every extreme that they name: `cache_lengths`: within each aligned group of 4 requests at most 2 have more than 256 cached tokens; in the first group exactly that many do, and some request has exactly 2048. parents[r, 0] = 0; for i >= 1, parents[r, i] lies between max(0, i - 8) and i - 1. `accepted_index`: each row lists 8 tree positions, each the parent of the next, ending at a position of 32 or more; where the root is reached the row repeats 0 at its front.
All inputs are finite; a program needn't handle non-finite values.
Results may differ from the reference program's by a relative error of at most 0.015.
The reference program's roundings to bfloat16 on the way count: a program that leaves them out, or rounds other values in their place, can miss the bound.
Values may be sent and summed in bfloat16 or wider, within the bound.
No kernel may reach another device: no remote copies, remote signals or barrier semaphores. Data moves between devices by JAX's collectives and lax.ppermute only.
A program may use at most 192 MiB of HBM per device.

```python
import jax
import jax.numpy as jnp
from jax import lax

D = 4096
HD = 128
QH = 32
KVH = 8
TREE = 64
PATH = 8
SHORT = 256
LONG = 2048
REQ_DEV = 4
REQUESTS = 32
TOKENS = 2048
CACHE_DEV = 4608
CACHE_ALL = 36864
PREFIX = 4096
N_TENSOR = 4


def draw_tree(key):
    position = jnp.arange(TREE, dtype=jnp.int32)
    lowest = jnp.maximum(position - 8, 0)
    highest = jnp.maximum(position, 1)
    return jax.random.randint(key, (REQUESTS, TREE), lowest[None, :], highest[None, :], dtype=jnp.int32)


def draw_parents(key, part):
    return draw_tree(jax.random.fold_in(key, 11))


def draw_accepted_index(key, part):
    parents = draw_tree(jax.random.fold_in(key, 11))
    current = jax.random.randint(jax.random.fold_in(key, 12), (REQUESTS,), TREE // 2, TREE, dtype=jnp.int32)
    chain_nodes = [current]
    for repeat in range(PATH - 1):
        current = jnp.take_along_axis(parents, current[:, None], axis=1)[:, 0]
        chain_nodes.append(current)
    return jnp.stack(chain_nodes[::-1], axis=1).astype(jnp.int32)


def draw_cache_lengths(key, part):
    groups = REQUESTS // REQ_DEV
    most_long = REQ_DEV // 2
    long_count = jax.random.randint(jax.random.fold_in(key, 21), (groups,), 0, most_long + 1, dtype=jnp.int32)
    long_count = long_count.at[0].set(most_long)
    ranking = jax.vmap(lambda subkey: jax.random.permutation(subkey, REQ_DEV))(jax.random.split(jax.random.fold_in(key, 22), groups))
    long_value = jax.random.randint(jax.random.fold_in(key, 23), (groups, REQ_DEV), 3 * LONG // 4, LONG + 1, dtype=jnp.int32)
    short_value = jax.random.randint(jax.random.fold_in(key, 24), (groups, REQ_DEV), SHORT // 2, SHORT + 1, dtype=jnp.int32)
    lengths = jnp.where(ranking < long_count[:, None], long_value, short_value)
    group_index = jnp.arange(groups, dtype=jnp.int32)[:, None]
    lengths = jnp.where((group_index == 0) & (ranking == 0), LONG, lengths)
    return lengths.reshape(REQUESTS).astype(jnp.int32)


def draw_cache_keys(key, part):
    shape = (CACHE_ALL, KVH * HD)
    return jnp.clip(jax.random.normal(jax.random.fold_in(key, 33), shape, jnp.float32), -5.0, 5.0).astype(jnp.bfloat16)


def set_ends(values, stream_key, least, high):
    index_at = [jax.random.randint(jax.random.fold_in(stream_key, axis), (), 0, length) for axis, length in enumerate(values.shape)]
    main_axis = values.shape.index(max(values.shape))
    beside = index_at[:main_axis] + [(index_at[main_axis] + 1) % values.shape[main_axis]] + index_at[main_axis + 1:]
    return values.at[tuple(index_at)].set(least).at[tuple(beside)].set(high)


def block_scale(own_key, extent, cuts, least, top_value):
    gain = 1.0
    for dim, shards_of in cuts:
        heights = jax.random.uniform(jax.random.fold_in(jax.random.fold_in(own_key, 6), dim), (shards_of,), jnp.float32, least / len(cuts), top_value / len(cuts))
        gain = gain * jnp.repeat(jnp.exp(heights), extent[dim] // shards_of).reshape((-1,) + (1,) * (len(extent) - 1 - dim))
    return gain


def noise(rng, shape, spread, most, cuts=(), kind=jnp.bfloat16):
    values = spread * jax.random.normal(rng, shape, jnp.float32)
    if cuts:
        values = values * block_scale(rng, shape, cuts, -0.22, 0.18)
    return jnp.clip(values, -most, most).astype(kind)


def setup_inputs(seed: int = 0) -> dict:
    seeds = jax.random.split(jax.random.key(seed), 15)
    return {
        "tokens": noise(seeds[0], (TOKENS, D), 1.0, 6.0, ((0, 32),)),
        "norm_gain": jnp.clip(1.0 + 0.18 * jax.random.normal(seeds[1], (D,), jnp.float32), 0.1, 1.9),
        "w_query": noise(seeds[2], (D, QH * HD), D ** -0.5, 0.09375, ((1, 4),)),
        "w_key": noise(seeds[3], (D, KVH * HD), (D // 9) ** -0.5, 0.25, ((1, 4),)),
        "w_value": noise(seeds[4], (D, KVH * HD), D ** -0.5, 0.09375, ((1, 4),)),
        "w_out": noise(seeds[5], (QH * HD, D), (QH * HD // 9) ** -0.5, 0.25, ((0, 4),)),
        "prefix_keys": noise(seeds[6], (PREFIX, KVH * HD), 1.0, 6.0, ((0, 8), (1, 4))),
        "prefix_values": noise(seeds[7], (PREFIX, KVH * HD), 1.0, 6.0, ((0, 8), (1, 4))),
        "cache_keys": draw_cache_keys(jax.random.fold_in(seeds[14], 71), 0),
        "cache_values": noise(seeds[9], (CACHE_ALL, KVH * HD), 1.0, 6.0, ((0, 8), (1, 4))),
        "cache_lengths": draw_cache_lengths(jax.random.fold_in(seeds[14], 71), 0),
        "prefix_used": set_ends(jax.random.randint(seeds[11], (REQUESTS,), PREFIX // 4, PREFIX + 1), jax.random.fold_in(seeds[11], 1), PREFIX // 4, PREFIX).astype(jnp.int32),
        "parents": draw_parents(jax.random.fold_in(seeds[14], 71), 0),
        "accepted_index": draw_accepted_index(jax.random.fold_in(seeds[14], 71), 0),
    }


NEG_FILL = -1e+30
HIGHEST = lax.Precision.HIGHEST

def rms_normed(tokens, norm_gain):
    values = tokens.astype(jnp.float32)
    factor = lax.rsqrt(lax.optimization_barrier(jnp.mean(values * values, axis=-1, keepdims=True)) + 1e-05)
    return (values * factor * norm_gain).astype(jnp.bfloat16)

def ancestor_table(parents):
    node_count = parents.shape[-1]
    column = jnp.arange(node_count, dtype=jnp.int32)
    linked = (parents[..., None] == column).astype(jnp.float32)
    itself = (column[:, None] == column[None, :]).astype(jnp.float32)
    ancestry = jnp.minimum(linked + itself, 1.0)
    for repeat in range(node_count.bit_length()):
        ancestry = jnp.minimum(jnp.einsum('rij,rjk->rik', ancestry, ancestry, precision=HIGHEST), 1.0)
    return ancestry

def rotate(values, positions):
    half_width = values.shape[-1] // 2
    frequency = 10000.0 ** (-jnp.arange(half_width, dtype=jnp.float32) / half_width)
    angles = positions.astype(jnp.float32)[:, None] * frequency[None, :]
    cosine = jnp.cos(angles)[:, None, :]
    sine_table = jnp.sin(angles)[:, None, :]
    first_half = values[..., :half_width]
    second_half = values[..., half_width:]
    return jnp.concatenate([first_half * cosine - second_half * sine_table, second_half * cosine + first_half * sine_table], axis=-1)

def reference(tokens, norm_gain, w_query, w_key, w_value, w_out, prefix_keys, prefix_values, cache_keys, cache_values, cache_lengths, prefix_used, parents, accepted_index):
    group_size = QH // KVH
    normed = rms_normed(tokens, norm_gain)
    query_raw = jnp.dot(normed, w_query, preferred_element_type=jnp.float32)
    key_raw = jnp.dot(normed, w_key, preferred_element_type=jnp.float32)
    value_raw = jnp.dot(normed, w_value, preferred_element_type=jnp.float32)
    ancestry = ancestor_table(parents)
    tree_depth = (lax.optimization_barrier(jnp.sum(ancestry, axis=-1)) - 1.0).astype(jnp.int32)
    position = ((prefix_used + cache_lengths)[:, None] + tree_depth).reshape(TOKENS)
    queries = rotate(query_raw.reshape(TOKENS, QH, HD), position).astype(jnp.bfloat16)
    queries = queries.reshape(REQUESTS, TREE, KVH, group_size, HD)
    new_keys = rotate(key_raw.reshape(TOKENS, KVH, HD), position).astype(jnp.bfloat16)
    new_keys = new_keys.reshape(REQUESTS, TREE, KVH * HD)
    new_values = value_raw.astype(jnp.bfloat16).reshape(REQUESTS, TREE, KVH * HD)
    accepted_keys = jnp.take_along_axis(new_keys, accepted_index[:, :, None], axis=1)
    accepted_values = jnp.take_along_axis(new_values, accepted_index[:, :, None], axis=1)
    per_group = cache_lengths.reshape(REQUESTS // REQ_DEV, REQ_DEV)
    group_base = (jnp.arange(REQUESTS // REQ_DEV, dtype=jnp.int32) * CACHE_DEV)[:, None]
    offset = (jnp.cumsum(per_group, axis=1) - per_group + group_base).reshape(REQUESTS).astype(jnp.int32)
    padding = jnp.zeros((LONG, KVH * HD), jnp.bfloat16)
    padded_keys = jnp.concatenate([cache_keys, padding], axis=0)
    padded_values = jnp.concatenate([cache_values, padding], axis=0)
    shared_keys = prefix_keys.reshape(PREFIX, KVH, HD)
    shared_values = prefix_values.reshape(PREFIX, KVH, HD)
    prefix_slots = jnp.arange(PREFIX, dtype=jnp.int32)
    cache_slots = jnp.arange(LONG, dtype=jnp.int32)

    def one_request(request_items):
        request_query, request_keys, request_values, request_table, request_offset, length, used = request_items
        corner = (request_offset.astype(jnp.int32), jnp.zeros((), jnp.int32))
        cached_keys = lax.dynamic_slice(padded_keys, corner, (LONG, KVH * HD)).reshape(LONG, KVH, HD)
        cached_values = lax.dynamic_slice(padded_values, corner, (LONG, KVH * HD)).reshape(LONG, KVH, HD)
        all_keys = jnp.concatenate([shared_keys, cached_keys, request_keys.reshape(TREE, KVH, HD)], axis=0).astype(jnp.float32)
        all_values = jnp.concatenate([shared_values, cached_values, request_values.reshape(TREE, KVH, HD)], axis=0).astype(jnp.float32)
        visible = jnp.concatenate([jnp.broadcast_to((prefix_slots < used)[None, :], (TREE, PREFIX)), jnp.broadcast_to((cache_slots < length)[None, :], (TREE, LONG)), request_table > 0.5], axis=1)
        score = jnp.einsum('ihgd,khd->hgik', request_query.astype(jnp.float32), all_keys) * HD ** (-0.5)
        masked = jnp.where(visible[None, None], score, NEG_FILL)
        largest = lax.optimization_barrier(jnp.max(masked, axis=-1, keepdims=True))
        weights = jnp.where(visible[None, None], jnp.exp(masked - largest), 0.0)
        denominator = lax.optimization_barrier(jnp.sum(weights, axis=-1))
        rounded_weights = lax.optimization_barrier(weights.astype(jnp.bfloat16)).astype(jnp.float32)
        numerator = jnp.einsum('hgik,khd->ihgd', rounded_weights, all_values)
        result = numerator / jnp.transpose(denominator, (2, 0, 1))[..., None]
        return result.astype(jnp.bfloat16).reshape(TREE, QH * HD)
    attended = lax.map(one_request, (queries, new_keys, new_values, ancestry, offset, cache_lengths, prefix_used))
    attended = attended.reshape(TOKENS, QH * HD)
    share = QH * HD // N_TENSOR
    summed = jnp.zeros((TOKENS, D), jnp.float32)
    for group in range(N_TENSOR):
        partial_value = jnp.dot(attended[:, group * share:(group + 1) * share], w_out[group * share:(group + 1) * share], preferred_element_type=jnp.float32)
        summed = summed + lax.optimization_barrier(partial_value.astype(jnp.bfloat16)).astype(jnp.float32)
    return (summed.astype(jnp.bfloat16), accepted_keys, accepted_values)
```

```python
import functools

import jax
import jax.numpy as jnp
from jax import lax
from jax.experimental import pallas as pl
from jax.experimental.pallas import tpu as pltpu
from jax.sharding import PartitionSpec as P

HD = 128
NEG_FILL = -1e30
LOG2E = 1.4426950408889634
AXES = ("batch", "tensor")
VMEM_LIMIT = 56 * 1024 * 1024


def params(**kw):
    return pltpu.CompilerParams(vmem_limit_bytes=VMEM_LIMIT, **kw)


def qkv_kernel(n_tok, steps, n_heads, kv_local, *refs):
    token_refs = refs[:n_tok]
    gain_ref, cos_ref, sin_ref, wq_ref, wk_ref, wv_ref = refs[n_tok : n_tok + 6]
    q_out, k_out, v_out = refs[n_tok + 6 : n_tok + 9]
    normed, acc = refs[n_tok + 9 :]
    step = pl.program_id(0)
    depth = wq_ref.shape[0]
    rows = token_refs[0].shape[0]
    q_cols = n_heads * HD
    k_cols = kv_local * HD

    @pl.when(step == 0)
    def _():
        for i, ref in enumerate(token_refs):
            values = ref[...].astype(jnp.float32)
            factor = lax.rsqrt(jnp.mean(values * values, axis=-1, keepdims=True) + 1e-05)
            scaled = (values * factor * gain_ref[...]).astype(jnp.bfloat16)
            for s in range(steps):
                normed[s, i * rows : (i + 1) * rows, :] = scaled[:, s * depth : (s + 1) * depth]

    x = normed[step]

    def part(lo, w_ref):
        width = w_ref.shape[1]
        d = jnp.dot(x, w_ref[...], preferred_element_type=jnp.float32)

        @pl.when(step == 0)
        def _():
            acc[:, lo : lo + width] = d

        @pl.when(step > 0)
        def _():
            acc[:, lo : lo + width] += d

    part(0, wq_ref)
    part(q_cols, wk_ref)
    part(q_cols + k_cols, wv_ref)

    @pl.when(step == steps - 1)
    def _():
        cosine = cos_ref[...]
        sine = sin_ref[...]
        reqs, tree = q_out.shape[0], q_out.shape[2]

        def rotated(lo):
            raw = acc[:, lo : lo + HD]
            return (raw * cosine + pltpu.roll(raw, HD // 2, 1) * sine).astype(jnp.bfloat16)

        for head in range(n_heads):
            out = rotated(head * HD)
            for r in range(reqs):
                q_out[r, head] = out[r * tree : (r + 1) * tree]
        for head in range(kv_local):
            k_out[:, head * HD : (head + 1) * HD] = rotated(q_cols + head * HD)
        v_out[...] = acc[:, q_cols + k_cols :].astype(jnp.bfloat16)


def project(token_list, gain, cosine, sine, w_query, w_key, w_value, reqs, tree):
    rows, width = token_list[0].shape
    total = rows * len(token_list)
    n_heads = w_query.shape[1] // HD
    kv_local = w_key.shape[1] // HD
    depth = min(512, width)
    steps = width // depth
    whole = lambda shape: pl.BlockSpec(shape, lambda s: (0,) * len(shape))
    return pl.pallas_call(
        functools.partial(qkv_kernel, len(token_list), steps, n_heads, kv_local),
        grid=(steps,),
        in_specs=[whole((rows, width)) for _ in token_list]
        + [whole((1, width)), whole((total, HD)), whole((total, HD))]
        + [pl.BlockSpec((depth, w.shape[1]), lambda s: (s, 0)) for w in (w_query, w_key, w_value)],
        out_specs=[
            whole((reqs, n_heads, tree, HD)),
            whole((total, w_key.shape[1])),
            whole((total, w_key.shape[1])),
        ],
        out_shape=[
            jax.ShapeDtypeStruct((reqs, n_heads, tree, HD), jnp.bfloat16),
            jax.ShapeDtypeStruct((total, w_key.shape[1]), jnp.bfloat16),
            jax.ShapeDtypeStruct((total, w_key.shape[1]), jnp.bfloat16),
        ],
        scratch_shapes=[
            pltpu.VMEM((steps, total, depth), jnp.bfloat16),
            pltpu.VMEM((total, w_query.shape[1] + 2 * w_key.shape[1]), jnp.float32),
        ],
        compiler_params=params(),
        cost_estimate=pl.CostEstimate(
            flops=2 * total * width * (w_query.shape[1] + 2 * w_key.shape[1]),
            bytes_accessed=2 * width * (w_query.shape[1] + 2 * w_key.shape[1]),
            transcendentals=0,
        ),
        name="project",
    )(*token_list, gain, cosine, sine, w_query, w_key, w_value)


def lane_max(t):
    return jnp.max(t, axis=1, keepdims=True)


def fold(q, k, v, bias, carry):
    scores = lax.dot_general(q, k, (((1,), (1,)), ((), ())), preferred_element_type=jnp.float32)
    t = scores * (HD**-0.5 * LOG2E) + bias
    keys = t.shape[1]
    rows = t.shape[0]
    m_block = jnp.broadcast_to(lane_max(t), (rows, HD))
    if carry is None:
        m_new = m_block
    else:
        m_old, l_old, acc_old = carry
        m_new = jnp.maximum(m_old, m_block)
    if keys % HD == 0:
        chunks = [jnp.exp2(t[:, j : j + HD] - m_new) for j in range(0, keys, HD)]
        total = chunks[0]
        for chunk in chunks[1:]:
            total = total + chunk
        p = jnp.concatenate([chunk.astype(jnp.bfloat16) for chunk in chunks], axis=1)
    else:
        p32 = jnp.exp2(t - m_new[:, :keys])
        total = jnp.broadcast_to(jnp.sum(p32, axis=1, keepdims=True), (rows, HD)) * (1.0 / HD)
        p = p32.astype(jnp.bfloat16)
    out = jnp.dot(p, v, preferred_element_type=jnp.float32)
    if carry is None:
        return m_new, total, out
    alpha = jnp.exp2(m_old - m_new)
    return m_new, l_old * alpha + total, acc_old * alpha + out


def cache_kernel(kv_local, block, lower, upper, q_ref, kn_ref, vn_ref, anc_ref, ck_ref, cv_ref, m_out, l_out, acc_out):
    r = pl.program_id(0)
    n_heads, tree = q_ref.shape[1], q_ref.shape[2]
    group = n_heads // kv_local
    rows = group * tree
    capacity = ck_ref.shape[0]
    bias = (anc_ref[0] - 1.0) * -NEG_FILL
    bias = jnp.concatenate([bias] * group, axis=0)
    for h in range(kv_local):
        cols = slice(h * HD, (h + 1) * HD)
        q = q_ref[0, h * group : (h + 1) * group].reshape(rows, HD)
        m, l, acc = fold(q, kn_ref[:, cols], vn_ref[:, cols], bias, None)
        m_out[0, h] = m
        l_out[0, h] = l
        acc_out[0, h] = acc
    low = lower[r]
    high = upper[r]
    first = (low // 16) * 16

    def step(i, _):
        begin = first + i * block
        start = pl.multiple_of(jnp.minimum(begin, capacity - block), 16)
        slots = start + lax.broadcasted_iota(jnp.int32, (1, block), 1)
        seen = (slots >= jnp.maximum(begin, low)) & (slots < high)
        mask = jnp.where(seen, 0.0, NEG_FILL)
        for h in range(kv_local):
            cols = slice(h * HD, (h + 1) * HD)
            q = q_ref[0, h * group : (h + 1) * group].reshape(rows, HD)
            k = ck_ref[pl.ds(start, block), cols]
            v = cv_ref[pl.ds(start, block), cols]
            m, l, acc = fold(q, k, v, mask, (m_out[0, h], l_out[0, h], acc_out[0, h]))
            m_out[0, h] = m
            l_out[0, h] = l
            acc_out[0, h] = acc
        return 0

    lax.fori_loop(0, (high - first + block - 1) // block, step, 0)


def state_shapes(reqs, kv_local, rows):
    return [jax.ShapeDtypeStruct((reqs, kv_local, rows, HD), jnp.float32)] * 3


def attend_cache(queries, new_keys, new_values, ancestry, cache_keys, cache_values, lower, upper, kv_local):
    reqs, n_heads, tree, _ = queries.shape
    rows = n_heads // kv_local * tree
    capacity, cols = cache_keys.shape
    block = min(512, capacity)
    state = pl.BlockSpec((1, kv_local, rows, HD), lambda r, *_: (r, 0, 0, 0))
    whole = pl.BlockSpec((capacity, cols), lambda r, *_: (0, 0))
    return pl.pallas_call(
        functools.partial(cache_kernel, kv_local, block),
        grid_spec=pltpu.PrefetchScalarGridSpec(
            num_scalar_prefetch=2,
            grid=(reqs,),
            in_specs=[
                pl.BlockSpec((1, n_heads, tree, HD), lambda r, *_: (r, 0, 0, 0)),
                pl.BlockSpec((tree, cols), lambda r, *_: (r, 0)),
                pl.BlockSpec((tree, cols), lambda r, *_: (r, 0)),
                pl.BlockSpec((1, tree, tree), lambda r, *_: (r, 0, 0)),
                whole,
                whole,
            ],
            out_specs=[state] * 3,
        ),
        out_shape=state_shapes(reqs, kv_local, rows),
        compiler_params=params(),
        cost_estimate=pl.CostEstimate(
            flops=4 * reqs * kv_local * rows * 1200 * HD, bytes_accessed=4 * capacity * cols, transcendentals=0
        ),
        name="attend_cache",
    )(lower, upper, queries, new_keys, new_values, ancestry, cache_keys, cache_values)


def prefix_kernel(kv_local, n_shards, final, bases, used, q_ref, *refs):
    r = pl.program_id(0)
    k_refs = refs[:n_shards]
    v_refs = refs[n_shards : 2 * n_shards]
    m_in, l_in, acc_in = refs[2 * n_shards : 2 * n_shards + 3]
    n_heads, tree = q_ref.shape[1], q_ref.shape[2]
    group = n_heads // kv_local
    rows = group * tree
    if final:
        out_ref, m_out, l_out, acc_out = refs[2 * n_shards + 3 :]
    else:
        m_out, l_out, acc_out = refs[2 * n_shards + 3 :]
    m_out[...] = m_in[...]
    l_out[...] = l_in[...]
    acc_out[...] = acc_in[...]
    for s in range(n_shards):
        count = k_refs[s].shape[0]
        visible = used[r] - bases[s]

        @pl.when(visible > 0)
        def _():
            slots = lax.broadcasted_iota(jnp.int32, (1, count), 1)
            mask = jnp.where(slots < visible, 0.0, NEG_FILL)
            for h in range(kv_local):
                cols = slice(h * HD, (h + 1) * HD)
                q = q_ref[0, h * group : (h + 1) * group].reshape(rows, HD)
                m, l, acc = fold(
                    q, k_refs[s][:, cols], v_refs[s][:, cols], mask, (m_out[0, h], l_out[0, h], acc_out[0, h])
                )
                m_out[0, h] = m
                l_out[0, h] = l
                acc_out[0, h] = acc

    if final:
        for h in range(kv_local):
            total = jnp.sum(l_out[0, h], axis=1, keepdims=True)
            result = (acc_out[0, h] / total).astype(jnp.bfloat16)
            for g in range(group):
                head = h * group + g
                out_ref[:, head * HD : (head + 1) * HD] = result[g * tree : (g + 1) * tree]


def attend_prefix(queries, keys, values, bases, used, state, kv_local, final):
    reqs, n_heads, tree, _ = queries.shape
    rows = n_heads // kv_local * tree
    n_shards = len(keys)
    spec = pl.BlockSpec((1, kv_local, rows, HD), lambda r, *_: (r, 0, 0, 0))
    count, cols = keys[0].shape
    shard = pl.BlockSpec((count, cols), lambda r, *_: (0, 0))
    if final:
        out_specs = pl.BlockSpec((tree, n_heads * HD), lambda r, *_: (r, 0))
        out_shape = jax.ShapeDtypeStruct((reqs * tree, n_heads * HD), jnp.bfloat16)
        scratch = [pltpu.VMEM((1, kv_local, rows, HD), jnp.float32)] * 3
        aliases = {}
    else:
        out_specs = [spec] * 3
        out_shape = state_shapes(reqs, kv_local, rows)
        scratch = []
        aliases = {3 + 2 * n_shards + i: i for i in range(3)}
    return pl.pallas_call(
        functools.partial(prefix_kernel, kv_local, n_shards, final),
        grid_spec=pltpu.PrefetchScalarGridSpec(
            num_scalar_prefetch=2,
            grid=(reqs,),
            in_specs=[pl.BlockSpec((1, n_heads, tree, HD), lambda r, *_: (r, 0, 0, 0))]
            + [shard] * (2 * n_shards)
            + [spec] * 3,
            out_specs=out_specs,
            scratch_shapes=scratch,
        ),
        out_shape=out_shape,
        input_output_aliases=aliases,
        compiler_params=params(),
        cost_estimate=pl.CostEstimate(
            flops=4 * reqs * kv_local * rows * n_shards * count * HD,
            bytes_accessed=2 * n_shards * count * cols * 2,
            transcendentals=0,
        ),
        name="attend_prefix",
    )(bases, used, queries, *keys, *values, *state)


def out_kernel(groups, x_ref, w_ref, *out_refs):
    product = jnp.dot(x_ref[...], w_ref[...], preferred_element_type=jnp.float32).astype(jnp.bfloat16)
    for out_ref, slots in zip(out_refs, groups):
        rows = out_ref.shape[1]
        for i, slot in enumerate(slots):
            out_ref[i] = product[slot * rows : (slot + 1) * rows]


def project_out(attended, w_out, groups, rows):
    depth, width = w_out.shape
    block = min(512, width)
    return pl.pallas_call(
        functools.partial(out_kernel, groups),
        grid=(width // block,),
        in_specs=[
            pl.BlockSpec(attended.shape, lambda j: (0, 0)),
            pl.BlockSpec((depth, block), lambda j: (0, j)),
        ],
        out_specs=[pl.BlockSpec((len(g), rows, block), lambda j: (0, 0, j)) for g in groups],
        out_shape=[jax.ShapeDtypeStruct((len(g), rows, width), jnp.bfloat16) for g in groups],
        compiler_params=params(),
        cost_estimate=pl.CostEstimate(
            flops=2 * attended.shape[0] * depth * width, bytes_accessed=2 * depth * width, transcendentals=0
        ),
        name="project_out",
    )(attended, w_out)


def ancestor_table(parents):
    node_count = parents.shape[-1]
    column = jnp.arange(node_count, dtype=jnp.int32)
    linked = (parents[..., None] == column) | (column[:, None] == column[None, :])
    ancestry = linked.astype(jnp.bfloat16)
    for repeat in range((node_count - 1).bit_length()):
        paths = jnp.einsum("rij,rjk->rik", ancestry, ancestry, preferred_element_type=jnp.float32)
        ancestry = jnp.minimum(paths, 1.0).astype(jnp.bfloat16)
    return ancestry.astype(jnp.float32)


def rotary_tables(position):
    half = HD // 2
    frequency = 10000.0 ** (-jnp.arange(half, dtype=jnp.float32) / half)
    angles = position.astype(jnp.float32)[:, None] * frequency[None, :]
    cosine = jnp.cos(angles)
    sine = jnp.sin(angles)
    return jnp.concatenate([cosine, cosine], axis=1), jnp.concatenate([-sine, sine], axis=1)


def swap_pairs(batch, tensor, move):
    columns = 2
    pairs = []
    for z in range(batch // columns):
        for x in range(columns):
            for t in range(tensor):
                z2, x2, t2 = move(z, x, t)
                pairs.append(((z * columns + x) * tensor + t, (z2 * columns + x2) * tensor + t2))
    return pairs


def body(
    sizes,
    tokens,
    norm_gain,
    w_query,
    w_key,
    w_value,
    w_out,
    prefix_keys,
    prefix_values,
    cache_keys,
    cache_values,
    cache_lengths,
    prefix_used,
    parents,
    accepted_index,
):
    batch, tensor = sizes
    reqs, tree = parents.shape
    kv_local = w_key.shape[1] // HD
    shard_rows = prefix_keys.shape[0]
    fast = sizes == (8, 4) and reqs == tensor and tokens.shape[0] == tree
    me_batch = lax.axis_index("batch")
    me_tensor = lax.axis_index("tensor")

    own_lengths = lax.dynamic_slice_in_dim(cache_lengths, me_batch * reqs, reqs)
    lower = jnp.cumsum(own_lengths) - own_lengths
    if fast:
        order = jnp.arange(reqs, dtype=jnp.int32) ^ me_tensor
        pick = order[:, None] == jnp.arange(reqs, dtype=jnp.int32)[None, :]
        sort1 = lambda a: jnp.sum(jnp.where(pick, a[None, :], 0), axis=1)
        own_lengths, lower, used = sort1(own_lengths), sort1(lower), sort1(prefix_used)
        tree_parents = jnp.sum(jnp.where(pick[:, :, None], parents[None], 0), axis=1)
    else:
        order = jnp.arange(reqs, dtype=jnp.int32)
        used = prefix_used
        tree_parents = parents

    if fast:
        pairs = functools.partial(swap_pairs, batch, tensor)
        core_pairs = pairs(lambda z, x, t: (z, x, t ^ 1))
        y_pairs = pairs(lambda z, x, t: (z, x, t ^ 2))
        x_pairs = pairs(lambda z, x, t: (z, 1 - x, t))
        z_pairs = pairs(lambda z, x, t: ((z + 1) % (batch // 2), x, t))
        send = lambda a, p: lax.ppermute(a, AXES, p)
        y_tokens = send(tokens, y_pairs)
        core_tokens = send(tokens, core_pairs)
        ring_keys, ring_values = [prefix_keys], [prefix_values]
        side_keys, side_values = [], []
        for s in range(batch // 2):
            if s < batch // 2 - 1:
                ring_keys.append(send(ring_keys[s], z_pairs))
                ring_values.append(send(ring_values[s], z_pairs))
            side_keys.append(send(ring_keys[s], x_pairs))
            side_values.append(send(ring_values[s], x_pairs))
        far_tokens = send(y_tokens, core_pairs)
        token_list = [tokens, core_tokens, y_tokens, far_tokens]
    else:
        gathered = lax.all_gather(tokens, "tensor", axis=0, tiled=True)
        token_list = [gathered]

    ancestry = ancestor_table(tree_parents)
    tree_depth = (jnp.sum(ancestry, axis=-1) - 1.0).astype(jnp.int32)
    position = ((used + own_lengths)[:, None] + tree_depth).reshape(reqs * tree)
    cosine, sine = rotary_tables(position)
    queries, new_keys, new_values = project(
        token_list, norm_gain[None, :], cosine, sine, w_query, w_key, w_value, reqs, tree
    )

    slot_of = jnp.arange(reqs, dtype=jnp.int32) ^ me_tensor if fast else order
    rows = (slot_of[:, None] * tree + accepted_index).reshape(-1)
    accepted_keys = jnp.take(new_keys, rows, axis=0).reshape(reqs, accepted_index.shape[1], -1)
    accepted_values = jnp.take(new_values, rows, axis=0).reshape(reqs, accepted_index.shape[1], -1)

    state = attend_cache(
        queries, new_keys, new_values, ancestry, cache_keys, cache_values, lower, lower + own_lengths, kv_local
    )
    if fast:
        z, x = me_batch // 2, me_batch % 2
        last = batch // 2 - 1
        for s in range(last + 1):
            home = (z - s) % (batch // 2)
            bases = jnp.stack([home * 2 + x, home * 2 + 1 - x]).astype(jnp.int32) * shard_rows
            state = attend_prefix(
                queries,
                [ring_keys[s], side_keys[s]],
                [ring_values[s], side_values[s]],
                bases,
                used,
                state,
                kv_local,
                s == last,
            )
        attended = state
        near, away = project_out(attended, w_out, ((0, 2), (1, 3)), tree)
        got = send(away, core_pairs)
        kept = near.astype(jnp.float32) + got.astype(jnp.float32)
        far = send(kept[1].astype(jnp.bfloat16), y_pairs)
        mixed_rows = (kept[0] + far.astype(jnp.float32)).astype(jnp.bfloat16)
    else:
        all_keys = lax.all_gather(prefix_keys, "batch", axis=0, tiled=True)
        all_values = lax.all_gather(prefix_values, "batch", axis=0, tiled=True)
        per_call = 4
        for s in range(0, batch, per_call):
            parts = range(s, min(s + per_call, batch))
            cut = lambda a: [a[i * shard_rows : (i + 1) * shard_rows] for i in parts]
            bases = jnp.array([i * shard_rows for i in parts], jnp.int32)
            state = attend_prefix(
                queries, cut(all_keys), cut(all_values), bases, used, state, kv_local, s + per_call >= batch
            )
        (partial,) = project_out(state, w_out, (tuple(range(reqs)),), tree)
        mixed_rows = lax.psum_scatter(
            partial.reshape(reqs * tree, -1), "tensor", scatter_dimension=0, tiled=True
        )
    return (mixed_rows, accepted_keys, accepted_values)


def solution(mesh):
    sizes = (mesh.shape["batch"], mesh.shape["tensor"])
    in_specs = (
        P(("batch", "tensor"), None),
        P(),
        P(None, "tensor"),
        P(None, "tensor"),
        P(None, "tensor"),
        P("tensor", None),
        P("batch", "tensor"),
        P("batch", "tensor"),
        P("batch", "tensor"),
        P("batch", "tensor"),
        P(),
        P("batch"),
        P("batch", None),
        P("batch", None),
    )
    out_specs = (
        P(("batch", "tensor"), None),
        P("batch", None, "tensor"),
        P("batch", None, "tensor"),
    )
    return jax.shard_map(
        functools.partial(body, sizes), mesh=mesh, in_specs=in_specs, out_specs=out_specs, check_vma=False
    )
```

```python
import functools

import jax
import jax.numpy as jnp
from jax import lax
from jax.experimental import pallas as pl
from jax.experimental.pallas import tpu as pltpu
from jax.sharding import PartitionSpec as P

HD = 128
NEG_FILL = -1e30
LOG2E = 1.4426950408889634
AXES = ("batch", "tensor")
SCALE = HD**-0.5 * LOG2E
COST = 1.1e9
HBM = pl.BlockSpec(memory_space=pltpu.HBM)
VMEM = pl.BlockSpec(memory_space=pltpu.VMEM)
SMEM = pl.BlockSpec(memory_space=pltpu.SMEM)


def call(kernel, in_specs, args, out_shape, scratch, megabytes, microseconds, name, after=()):
    n_in, n_out = len(args), len(out_shape)

    def wrapped(*refs):
        kernel(*refs[:n_in], *refs[n_in + len(after) :])

    return pl.pallas_call(
        wrapped,
        in_specs=in_specs + [HBM] * len(after),
        out_specs=[VMEM] * n_out,
        out_shape=out_shape,
        scratch_shapes=scratch,
        compiler_params=pltpu.CompilerParams(vmem_limit_bytes=megabytes * 2**20),
        cost_estimate=pl.CostEstimate(flops=int(microseconds * COST), bytes_accessed=0, transcendentals=0),
        name=name,
    )(*args, *after)


def dot_nt(a, b):
    return lax.dot_general(a, b, (((1,), (1,)), ((), ())), preferred_element_type=jnp.float32)


def head_cols(h):
    return slice(h * HD, (h + 1) * HD)


def fetch_all(sources, held, sems):
    copies = [pltpu.make_async_copy(src, held.at[i], sems.at[i]) for i, src in enumerate(sources)]
    for copy in copies:
        copy.start()
    return copies


def qkv_kernel(n_tok, n_heads, kv_local, steps, *refs):
    token_refs = refs[:n_tok]
    gain_ref, cos_ref, sin_ref = refs[n_tok : n_tok + 3]
    weights = refs[n_tok + 3 : n_tok + 6]
    q_out, k_out, v_out, held, normed, acc, wq, wk, wv, sems, weight_sems = refs[n_tok + 6 :]
    copies = fetch_all(token_refs, held, sems)
    depth = wq.shape[0] // steps
    chunks = []
    for s in range(steps):
        span = slice(s * depth, (s + 1) * depth)
        chunks.append(
            [
                pltpu.make_async_copy(src.at[span], dst.at[span], weight_sems.at[s, i])
                for i, (src, dst) in enumerate(zip(weights, (wq, wk, wv)))
            ]
        )
        for copy in chunks[-1]:
            copy.start()
    rows = held.shape[1]
    step = min(16, rows)
    for i in range(n_tok):
        copies[i].wait()
        for lo in range(0, rows, step):
            values = held[i, lo : lo + step].astype(jnp.float32)
            factor = lax.rsqrt(jnp.mean(values * values, axis=-1, keepdims=True) + 1e-05)
            normed[i * rows + lo : i * rows + lo + step] = (values * factor * gain_ref[...]).astype(jnp.bfloat16)
    cosine = cos_ref[...]
    sine = sin_ref[...]
    reqs, tree = q_out.shape[0], q_out.shape[2]

    def rotated(raw):
        return (raw * cosine + pltpu.roll(raw, HD // 2, 1) * sine).astype(jnp.bfloat16)

    for s in range(steps):
        for copy in chunks[s]:
            copy.wait()
        span = slice(s * depth, (s + 1) * depth)
        x = normed[:, span]
        lo = 0
        for which, w in enumerate((wq, wk, wv)):
            width = w.shape[1]
            raw = jnp.dot(x, w[span], preferred_element_type=jnp.float32)
            if s > 0:
                raw = acc[:, lo : lo + width] + raw
            if s < steps - 1:
                acc[:, lo : lo + width] = raw
            elif which == 0:
                for head in range(n_heads):
                    out = rotated(raw[:, head_cols(head)])
                    for r in range(reqs):
                        q_out[r, head] = out[r * tree : (r + 1) * tree]
            elif which == 1:
                for head in range(kv_local):
                    k_out[:, head_cols(head)] = rotated(raw[:, head_cols(head)])
            else:
                v_out[...] = raw.astype(jnp.bfloat16)
            lo += width


def project(token_list, gain, cosine, sine, w_query, w_key, w_value, tree, after=()):
    rows, width = token_list[0].shape
    n_tok = len(token_list)
    total = rows * n_tok
    n_heads = w_query.shape[1] // HD
    cols = w_key.shape[1]
    steps = 4
    return call(
        functools.partial(qkv_kernel, n_tok, n_heads, cols // HD, steps),
        [HBM] * n_tok + [VMEM] * 3 + [HBM] * 3,
        [*token_list, gain, cosine, sine, w_query, w_key, w_value],
        [
            jax.ShapeDtypeStruct((total // tree, n_heads, tree, HD), jnp.bfloat16),
            jax.ShapeDtypeStruct((total, cols), jnp.bfloat16),
            jax.ShapeDtypeStruct((total, cols), jnp.bfloat16),
        ],
        [
            pltpu.VMEM((n_tok, rows, width), jnp.bfloat16),
            pltpu.VMEM((total, width), jnp.bfloat16),
            pltpu.VMEM((total, w_query.shape[1] + 2 * cols), jnp.float32),
            pltpu.VMEM(w_query.shape, jnp.bfloat16),
            pltpu.VMEM(w_key.shape, jnp.bfloat16),
            pltpu.VMEM(w_value.shape, jnp.bfloat16),
            pltpu.SemaphoreType.DMA((n_tok,)),
            pltpu.SemaphoreType.DMA((steps, 3)),
        ],
        50,
        7,
        "project",
        after,
    )


def absorb(carry, scores, biases, v):
    chunks = []
    for s, bias in zip(scores, biases):
        s = s + bias
        chunks += [s[:, j : j + HD] for j in range(0, s.shape[1], HD)]
    top = chunks[0]
    for c in chunks[1:]:
        top = jnp.maximum(top, c)
    m_new = jnp.broadcast_to(jnp.max(top, axis=1, keepdims=True) * SCALE, top.shape)
    if carry is not None:
        m_new = jnp.maximum(carry[0], m_new)
    total = None
    rounded = []
    for c in chunks:
        w = jnp.exp2(c * SCALE - m_new)
        total = w if total is None else total + w
        rounded.append(w.astype(jnp.bfloat16))
    out = jnp.dot(jnp.concatenate(rounded, axis=1), v, preferred_element_type=jnp.float32)
    if carry is not None:
        alpha = jnp.exp2(carry[0] - m_new)
        total = carry[1] * alpha + total
        out = carry[2] * alpha + out
    return m_new, total, out


def fold_heads(q_ref, slot, kv_local, keys, values, bias, load, store):
    group, tree = q_ref.shape[1] // kv_local, q_ref.shape[2]
    rows = group * tree

    def scores_of(h):
        q = q_ref[slot, h * group : (h + 1) * group].reshape(rows, HD)
        return [dot_nt(q, k(h)) for k in keys]

    def values_of(h):
        parts = [v(h) for v in values]
        return parts[0] if len(parts) == 1 else jnp.concatenate(parts, axis=0)

    ahead = scores_of(0)
    for h in range(kv_local):
        now = ahead
        if h + 1 < kv_local:
            ahead = scores_of(h + 1)
        store(h, absorb(load(h), now, bias, values_of(h)))


def state_access(refs, r):
    def load(h):
        return tuple(ref[r, h] for ref in refs)

    def store(h, state):
        for ref, value in zip(refs, state):
            ref[r, h] = value

    return load, store


def fold_shards(q_ref, r, offset, kv_local, used, bases, base0, held, groups, states):
    n = held.shape[0] // 2
    count = held.shape[1]
    load, store = state_access(states, r)
    for group in groups:
        visible = [used - bases[base0 + i] for i in group]
        most = visible[0]
        for other in visible[1:]:
            most = jnp.maximum(most, other)

        @pl.when(most > 0)
        def _():
            slots = lax.broadcasted_iota(jnp.int32, (1, count), 1)
            fold_heads(
                q_ref,
                offset + r,
                kv_local,
                [lambda h, i=i: held[i, :, head_cols(h)] for i in group],
                [lambda h, i=i: held[n + i, :, head_cols(h)] for i in group],
                [jnp.where(slots < v, 0.0, NEG_FILL) for v in visible],
                load,
                store,
            )


def pairs_of(n):
    return [tuple(range(i, min(i + 2, n))) for i in range(0, n, 2)]


def first_kernel(kv_local, near, block, n_shards, offset, groups, base0, info, bases, q_ref, kn_ref, vn_ref, anc_ref, ck_ref, cv_ref, *refs):
    sources = refs[: 2 * n_shards]
    m_out, l_out, acc_out, k_near, v_near, held, sems = refs[-7:]
    states = (m_out, l_out, acc_out)
    copies = fetch_all(sources, held, sems)
    reqs = m_out.shape[0]
    n_heads, tree = q_ref.shape[1:3]
    group = n_heads // kv_local
    capacity = ck_ref.shape[0]
    for r in range(reqs):
        load, store = state_access(states, r)
        low = info[0, offset + r]
        high = info[1, offset + r]
        start0 = pl.multiple_of(jnp.minimum((low // 16) * 16, capacity - near), 16)
        k_near[0:tree] = kn_ref[(offset + r) * tree : (offset + r + 1) * tree]
        v_near[0:tree] = vn_ref[(offset + r) * tree : (offset + r + 1) * tree]
        k_near[tree : tree + near] = ck_ref[pl.ds(start0, near), :]
        v_near[tree : tree + near] = cv_ref[pl.ds(start0, near), :]
        column = lax.broadcasted_iota(jnp.int32, (tree, tree + near), 1)
        slots = column - tree + start0
        seen = ((slots >= low) & (slots < high)).astype(jnp.float32)
        linked = jnp.concatenate([anc_ref[offset + r], jnp.zeros((tree, tree + near - HD), jnp.float32)], axis=1)
        bias = jnp.where(jnp.where(column < tree, linked, seen) > 0.5, 0.0, NEG_FILL)
        bias = jnp.concatenate([bias] * group, axis=0)
        fold_heads(
            q_ref,
            offset + r,
            kv_local,
            [lambda h: k_near[:, head_cols(h)]],
            [lambda h: v_near[:, head_cols(h)]],
            [bias],
            lambda h: None,
            store,
        )
        begin0 = start0 + near

        def step(i, _):
            begin = begin0 + i * block
            start = pl.multiple_of(jnp.minimum(begin, capacity - block), 16)
            place = start + lax.broadcasted_iota(jnp.int32, (1, block), 1)
            mask = jnp.where((place >= begin) & (place < high), 0.0, NEG_FILL)
            fold_heads(
                q_ref,
                offset + r,
                kv_local,
                [lambda h: ck_ref[pl.ds(start, block), head_cols(h)]],
                [lambda h: cv_ref[pl.ds(start, block), head_cols(h)]],
                [mask],
                load,
                store,
            )
            return 0

        lax.fori_loop(0, (jnp.maximum(high - begin0, 0) + block - 1) // block, step, 0)
    for copy in copies:
        copy.wait()
    for r in range(reqs):
        fold_shards(q_ref, r, offset, kv_local, info[2, offset + r], bases, base0, held, groups, states)


def state_shapes(reqs, kv_local, rows):
    return [jax.ShapeDtypeStruct((reqs, kv_local, rows, HD), jnp.float32)] * 3


def shard_scratch(shards):
    n = 2 * len(shards)
    return [pltpu.VMEM((n,) + shards[0][0].shape, jnp.bfloat16), pltpu.SemaphoreType.DMA((n,))]


def flat(shards):
    return [k for k, _ in shards] + [v for _, v in shards]


def attend_first(parts, ancestry, cache_keys, cache_values, info, bases, shards, span, offset, reqs, after=()):
    queries, new_keys, new_values = parts
    shards = shards[span[0] : span[1]]
    _, n_heads, tree, _ = queries.shape
    capacity, cols = cache_keys.shape
    kv_local = cols // HD
    near = min(384 - tree, capacity)
    block = min(896, capacity)
    n = len(shards)
    return call(
        functools.partial(first_kernel, kv_local, near, block, n, offset, pairs_of(n), span[0]),
        [SMEM] * 2 + [VMEM] * 6 + [HBM] * (2 * n),
        [info, bases, queries, new_keys, new_values, ancestry, cache_keys, cache_values, *flat(shards)],
        state_shapes(reqs, kv_local, n_heads // kv_local * tree),
        [pltpu.VMEM((tree + near, cols), jnp.bfloat16)] * 2 + shard_scratch(shards),
        40,
        6,
        "attend_first",
        after,
    )


def middle_kernel(kv_local, n_shards, offset, groups, base0, info, bases, q_ref, *refs):
    sources = refs[: 2 * n_shards]
    ins = refs[2 * n_shards : 2 * n_shards + 3]
    outs = refs[2 * n_shards + 3 : 2 * n_shards + 6]
    held, sems = refs[2 * n_shards + 6 :]
    copies = fetch_all(sources, held, sems)
    for src, dst in zip(ins, outs):
        dst[...] = src[...]
    for copy in copies:
        copy.wait()
    for r in range(outs[0].shape[0]):
        fold_shards(q_ref, r, offset, kv_local, info[2, offset + r], bases, base0, held, groups, outs)


def attend_middle(queries, info, bases, shards, span, state, offset, after=()):
    shards = shards[span[0] : span[1]]
    reqs = state[0].shape[0]
    _, n_heads, tree, _ = queries.shape
    kv_local = shards[0][0].shape[1] // HD
    n = len(shards)
    return call(
        functools.partial(middle_kernel, kv_local, n, offset, pairs_of(n), span[0]),
        [SMEM] * 2 + [VMEM] + [HBM] * (2 * n) + [VMEM] * 3,
        [info, bases, queries, *flat(shards), *state],
        state_shapes(reqs, kv_local, n_heads // kv_local * tree),
        shard_scratch(shards),
        40,
        1.5 + 0.4 * n * reqs,
        "attend_middle",
        after,
    )


def last_kernel(kv_local, n_shards, offset, groups, base0, block, info, bases, q_ref, *refs):
    sources = refs[: 2 * n_shards]
    ins = refs[2 * n_shards : 2 * n_shards + 3]
    w_ref = refs[2 * n_shards + 3]
    m_s, l_s, acc_s, attended, w_held, w_sems, held, sems = refs[-8:]
    reqs = m_s.shape[0]
    n_heads, tree = q_ref.shape[1:3]
    outs = refs[-8 - reqs : -8]
    states = (m_s, l_s, acc_s)
    group = n_heads // kv_local
    copies = fetch_all(sources, held, sems)
    cuts = [slice(lo, lo + block) for lo in range(0, w_ref.shape[1], block)]
    w_copies = fetch_all([w_ref.at[:, cut] for cut in cuts], w_held, w_sems)
    for src, dst in zip(ins, states):
        dst[...] = src[...]
    for copy in copies:
        copy.wait()
    for r in range(reqs):
        fold_shards(q_ref, r, offset, kv_local, info[2, offset + r], bases, base0, held, groups, states)
        for h in range(kv_local):
            total = jnp.sum(l_s[r, h], axis=1, keepdims=True)
            result = (acc_s[r, h] / total).astype(jnp.bfloat16)
            for g in range(group):
                attended[r, :, head_cols(h * group + g)] = result[g * tree : (g + 1) * tree]
    x = attended[...].reshape(reqs * tree, n_heads * HD)
    for i, cut in enumerate(cuts):
        w_copies[i].wait()
        product = jnp.dot(x, w_held[i], preferred_element_type=jnp.float32).astype(jnp.bfloat16)
        for r in range(reqs):
            outs[r][:, cut] = product[r * tree : (r + 1) * tree]


def attend_last(queries, info, bases, shards, span, state, w_out, offset, after=()):
    shards = shards[span[0] : span[1]]
    reqs = state[0].shape[0]
    _, n_heads, tree, _ = queries.shape
    kv_local = shards[0][0].shape[1] // HD
    rows = n_heads // kv_local * tree
    n = len(shards)
    depth, width = w_out.shape
    block = min(1024, width)
    return call(
        functools.partial(last_kernel, kv_local, n, offset, pairs_of(n), span[0], block),
        [SMEM] * 2 + [VMEM] + [HBM] * (2 * n) + [VMEM] * 3 + [HBM],
        [info, bases, queries, *flat(shards), *state, w_out],
        [jax.ShapeDtypeStruct((tree, width), jnp.bfloat16)] * reqs,
        [pltpu.VMEM((reqs, kv_local, rows, HD), jnp.float32)] * 3
        + [
            pltpu.VMEM((reqs, tree, n_heads * HD), jnp.bfloat16),
            pltpu.VMEM((width // block, depth, block), jnp.bfloat16),
            pltpu.SemaphoreType.DMA((width // block,)),
        ]
        + shard_scratch(shards),
        50,
        3.5 + 0.4 * n * reqs,
        "attend_last",
        after,
    )


def add_kernel(*refs):
    total = refs[0][...].astype(jnp.float32)
    for ref in refs[1:-1]:
        total = total + ref[...].astype(jnp.float32)
    refs[-1][...] = total.astype(refs[-1].dtype)


def add_up(*terms, dtype=jnp.bfloat16):
    outs = call(
        add_kernel,
        [VMEM] * len(terms),
        list(terms),
        [jax.ShapeDtypeStruct(terms[0].shape, dtype)],
        [],
        8,
        1,
        "add_up",
    )
    return outs[0]


def ancestor_table(parents):
    node_count = parents.shape[-1]
    column = jnp.arange(node_count, dtype=jnp.int32)
    linked = (parents[..., None] == column) | (column[:, None] == column[None, :])
    ancestry = linked.astype(jnp.bfloat16)
    for repeat in range((node_count - 1).bit_length()):
        paths = jnp.einsum("rij,rjk->rik", ancestry, ancestry, preferred_element_type=jnp.float32)
        ancestry = jnp.minimum(paths, 1.0).astype(jnp.bfloat16)
    return ancestry.astype(jnp.float32)


def rotary_tables(position):
    half = HD // 2
    frequency = 10000.0 ** (-jnp.arange(half, dtype=jnp.float32) / half)
    angles = position.astype(jnp.float32)[:, None] * frequency[None, :]
    cosine = jnp.cos(angles)
    sine = jnp.sin(angles)
    return jnp.concatenate([cosine, cosine], axis=1), jnp.concatenate([-sine, sine], axis=1)


def swap_pairs(batch, tensor, move):
    columns = 2
    pairs = []
    for z in range(batch // columns):
        for x in range(columns):
            for t in range(tensor):
                z2, x2, t2 = move(z, x, t)
                pairs.append(((z * columns + x) * tensor + t, (z2 * columns + x2) * tensor + t2))
    return pairs


def body(
    sizes,
    tokens,
    norm_gain,
    w_query,
    w_key,
    w_value,
    w_out,
    prefix_keys,
    prefix_values,
    cache_keys,
    cache_values,
    cache_lengths,
    prefix_used,
    parents,
    accepted_index,
):
    batch, tensor = sizes
    reqs, tree = parents.shape
    shard_rows = prefix_keys.shape[0]
    fast = sizes == (8, 4) and reqs == tensor and tokens.shape[0] == tree
    me_batch = lax.axis_index("batch")
    me_tensor = lax.axis_index("tensor")
    slots = jnp.arange(reqs, dtype=jnp.int32)

    if fast:
        pairs = functools.partial(swap_pairs, batch, tensor)
        core_pairs = pairs(lambda z, x, t: (z, x, t ^ 1))
        y_pairs = pairs(lambda z, x, t: (z, x, t ^ 2))
        x_pairs = pairs(lambda z, x, t: (z, 1 - x, t))
        z_pairs = pairs(lambda z, x, t: ((z + 1) % (batch // 2), x, t))
        send = lambda a, p: lax.ppermute(a, AXES, p)
        core_tokens = send(tokens, core_pairs)
        y_tokens = send(tokens, y_pairs)
        far_tokens = send(y_tokens, core_pairs)
    order = slots ^ me_tensor if fast else slots
    pick = order[:, None] == slots[None, :]
    own_lengths = lax.dynamic_slice_in_dim(cache_lengths, me_batch * reqs, reqs)
    lower = jnp.cumsum(own_lengths) - own_lengths
    table = jnp.stack([lower, lower + own_lengths, prefix_used])
    info = jnp.sum(jnp.where(pick[None], table[:, None, :], 0), axis=2)
    tree_parents = jnp.sum(jnp.where(pick[:, :, None], parents[None], 0), axis=1)
    ancestry = ancestor_table(tree_parents)
    tree_depth = (jnp.sum(ancestry, axis=-1) - 1.0).astype(jnp.int32)
    position = ((info[2] + info[1] - info[0])[:, None] + tree_depth).reshape(reqs * tree)
    if fast:
        steps = batch // 2
        own_keys, own_values, _ = lax.optimization_barrier((prefix_keys, prefix_values, own_lengths))
        ring = [(prefix_keys, prefix_values)]
        ring.append((send(own_keys, z_pairs), send(own_values, z_pairs)))
        side = [(send(own_keys, x_pairs), send(own_values, x_pairs))]
    cosine, sine = rotary_tables(position)
    ancestry = jnp.pad(ancestry, ((0, 0), (0, 0), (0, HD - tree)))
    shard_ids = jnp.arange(batch, dtype=jnp.int32)
    if fast:
        z, x = me_batch // 2, me_batch % 2
        shard_ids = (z - shard_ids // 2) % (batch // 2) * 2 + (x ^ (shard_ids % 2))
    bases = (shard_ids * shard_rows).astype(jnp.int32)

    def projected(token_list, after=()):
        return project(token_list, norm_gain[None, :], cosine, sine, w_query, w_key, w_value, tree, after)

    if fast:
        def pass_on(step, after):
            keys, values, _ = lax.optimization_barrier((*ring[step], after))
            if step < steps - 1:
                ring.append((send(keys, z_pairs), send(values, z_pairs)))
                side.append((send(keys, x_pairs), send(values, x_pairs)))
            else:
                side.append((send(keys, x_pairs), send(side[-1][1], z_pairs)))

        pass_on(1, cosine)
        parts = projected([tokens, core_tokens, y_tokens, far_tokens])
        queries, new_keys, new_values = parts
        pass_on(2, queries)
        shards = [shard for s in range(steps - 1) for shard in (ring[s], side[s])]
        first = functools.partial(
            attend_first,
            (queries, new_keys, new_values),
            ancestry,
            cache_keys,
            cache_values,
            info,
            bases,
            shards,
            (0, 2),
            reqs=2,
        )
        far_state = first(offset=2)
        pass_on(steps - 1, far_state[0])
        shards += [ring[-1], side[-1]]
        n = len(shards)
        far_state = attend_middle(queries, info, bases, shards, (2, 5), far_state, 2)
        near_state = first(offset=0, after=far_state[:1])
        far_state = attend_middle(queries, info, bases, shards, (5, n - 1), far_state, 2, near_state[:1])
        kept, away = attend_last(queries, info, bases, shards, (n - 1, n), far_state, w_out, 2)
        got = send(away, core_pairs)
        summed = add_up(kept, got)
        far = send(summed, y_pairs)
        kept, away = attend_last(queries, info, bases, shards, (2, n), near_state, w_out, 0, (summed,))
        got = send(away, core_pairs)
        mixed_rows = add_up(add_up(kept, far, dtype=jnp.float32), got)
    else:
        gathered = lax.all_gather(tokens, "tensor", axis=0, tiled=True)
        parts = projected([gathered])
        queries, new_keys, new_values = parts
        all_keys = lax.all_gather(prefix_keys, "batch", axis=0, tiled=True)
        all_values = lax.all_gather(prefix_values, "batch", axis=0, tiled=True)
        split = lambda a: [a[i * shard_rows : (i + 1) * shard_rows] for i in range(batch)]
        shards = list(zip(split(all_keys), split(all_values)))
        state = attend_first(parts, ancestry, cache_keys, cache_values, info, bases, shards, (0, 2), 0, reqs)
        for s in range(2, batch - 2, 4):
            state = attend_middle(queries, info, bases, shards, (s, min(s + 4, batch - 2)), state, 0)
        partial = attend_last(queries, info, bases, shards, (batch - 2, batch), state, w_out, 0)
        mixed_rows = lax.psum_scatter(
            jnp.concatenate(partial, axis=0), "tensor", scatter_dimension=0, tiled=True
        )
    rows = ((slots ^ me_tensor if fast else slots)[:, None] * tree + accepted_index).reshape(-1)
    accepted_keys = jnp.take(new_keys, rows, axis=0).reshape(reqs, accepted_index.shape[1], -1)
    accepted_values = jnp.take(new_values, rows, axis=0).reshape(reqs, accepted_index.shape[1], -1)
    return (mixed_rows, accepted_keys, accepted_values)


def solution(mesh):
    sizes = (mesh.shape["batch"], mesh.shape["tensor"])
    in_specs = (
        P(("batch", "tensor"), None),
        P(),
        P(None, "tensor"),
        P(None, "tensor"),
        P(None, "tensor"),
        P("tensor", None),
        P("batch", "tensor"),
        P("batch", "tensor"),
        P("batch", "tensor"),
        P("batch", "tensor"),
        P(),
        P("batch"),
        P("batch", None),
        P("batch", None),
    )
    out_specs = (
        P(("batch", "tensor"), None),
        P("batch", None, "tensor"),
        P("batch", None, "tensor"),
    )
    return jax.shard_map(
        functools.partial(body, sizes), mesh=mesh, in_specs=in_specs, out_specs=out_specs, check_vma=False
    )
```

```python
import functools

import jax
import jax.numpy as jnp
from jax import lax
from jax.experimental import pallas as pl
from jax.experimental.pallas import tpu as pltpu
from jax.sharding import PartitionSpec as P

HD = 128
NEG_FILL = -1e30
LOG2E = 1.4426950408889634
AXES = ("batch", "tensor")
SCALE = HD**-0.5 * LOG2E
COST = 1.1e9
HBM = pl.BlockSpec(memory_space=pltpu.HBM)
VMEM = pl.BlockSpec(memory_space=pltpu.VMEM)
SMEM = pl.BlockSpec(memory_space=pltpu.SMEM)


def call(kernel, in_specs, args, out_shape, scratch, megabytes, microseconds, name, after=()):
    n_in, n_out = len(args), len(out_shape)

    def wrapped(*refs):
        kernel(*refs[:n_in], *refs[n_in + len(after) :])

    return pl.pallas_call(
        wrapped,
        in_specs=in_specs + [HBM] * len(after),
        out_specs=[VMEM] * n_out,
        out_shape=out_shape,
        scratch_shapes=scratch,
        compiler_params=pltpu.CompilerParams(vmem_limit_bytes=megabytes * 2**20),
        cost_estimate=pl.CostEstimate(flops=int(microseconds * COST), bytes_accessed=0, transcendentals=0),
        name=name,
    )(*args, *after)


def dot_nt(a, b):
    return lax.dot_general(a, b, (((1,), (1,)), ((), ())), preferred_element_type=jnp.float32)


def head_cols(h):
    return slice(h * HD, (h + 1) * HD)


def fetch_all(sources, held, sems):
    copies = [pltpu.make_async_copy(src, held.at[i], sems.at[i]) for i, src in enumerate(sources)]
    for copy in copies:
        copy.start()
    return copies


def qkv_kernel(n_tok, n_heads, kv_local, steps, *refs):
    token_refs = refs[:n_tok]
    gain_ref, cos_ref, sin_ref = refs[n_tok : n_tok + 3]
    weights = refs[n_tok + 3 : n_tok + 6]
    q_out, k_out, v_out, held, normed, acc, wq, wk, wv, sems, weight_sems = refs[n_tok + 6 :]
    copies = fetch_all(token_refs, held, sems)
    depth = wq.shape[0] // steps
    chunks = []
    for s in range(steps):
        span = slice(s * depth, (s + 1) * depth)
        chunks.append(
            [
                pltpu.make_async_copy(src.at[span], dst.at[span], weight_sems.at[s, i])
                for i, (src, dst) in enumerate(zip(weights, (wq, wk, wv)))
            ]
        )
        for copy in chunks[-1]:
            copy.start()
    rows = held.shape[1]
    step = min(16, rows)
    for i in range(n_tok):
        copies[i].wait()
        for lo in range(0, rows, step):
            values = held[i, lo : lo + step].astype(jnp.float32)
            factor = lax.rsqrt(jnp.mean(values * values, axis=-1, keepdims=True) + 1e-05)
            normed[i * rows + lo : i * rows + lo + step] = (values * factor * gain_ref[...]).astype(jnp.bfloat16)
    cosine = cos_ref[...]
    sine = sin_ref[...]
    reqs, tree = q_out.shape[0], q_out.shape[2]

    def rotated(raw):
        return (raw * cosine + pltpu.roll(raw, HD // 2, 1) * sine).astype(jnp.bfloat16)

    for s in range(steps):
        for copy in chunks[s]:
            copy.wait()
        span = slice(s * depth, (s + 1) * depth)
        x = normed[:, span]
        lo = 0
        for which, w in enumerate((wq, wk, wv)):
            width = w.shape[1]
            raw = jnp.dot(x, w[span], preferred_element_type=jnp.float32)
            if s > 0:
                raw = acc[:, lo : lo + width] + raw
            if s < steps - 1:
                acc[:, lo : lo + width] = raw
            elif which == 0:
                for head in range(n_heads):
                    out = rotated(raw[:, head_cols(head)])
                    for r in range(reqs):
                        q_out[r, head] = out[r * tree : (r + 1) * tree]
            elif which == 1:
                for head in range(kv_local):
                    k_out[:, head_cols(head)] = rotated(raw[:, head_cols(head)])
            else:
                v_out[...] = raw.astype(jnp.bfloat16)
            lo += width


def project(token_list, gain, cosine, sine, w_query, w_key, w_value, tree, after=()):
    rows, width = token_list[0].shape
    n_tok = len(token_list)
    total = rows * n_tok
    n_heads = w_query.shape[1] // HD
    cols = w_key.shape[1]
    steps = 4
    return call(
        functools.partial(qkv_kernel, n_tok, n_heads, cols // HD, steps),
        [HBM] * n_tok + [VMEM] * 3 + [HBM] * 3,
        [*token_list, gain, cosine, sine, w_query, w_key, w_value],
        [
            jax.ShapeDtypeStruct((total // tree, n_heads, tree, HD), jnp.bfloat16),
            jax.ShapeDtypeStruct((total, cols), jnp.bfloat16),
            jax.ShapeDtypeStruct((total, cols), jnp.bfloat16),
        ],
        [
            pltpu.VMEM((n_tok, rows, width), jnp.bfloat16),
            pltpu.VMEM((total, width), jnp.bfloat16),
            pltpu.VMEM((total, w_query.shape[1] + 2 * cols), jnp.float32),
            pltpu.VMEM(w_query.shape, jnp.bfloat16),
            pltpu.VMEM(w_key.shape, jnp.bfloat16),
            pltpu.VMEM(w_value.shape, jnp.bfloat16),
            pltpu.SemaphoreType.DMA((n_tok,)),
            pltpu.SemaphoreType.DMA((steps, 3)),
        ],
        50,
        7,
        "project",
        after,
    )


def absorb(carry, scores, biases, v):
    chunks = []
    for s, bias in zip(scores, biases):
        s = s + bias
        chunks += [s[:, j : j + HD] for j in range(0, s.shape[1], HD)]
    top = chunks[0]
    for c in chunks[1:]:
        top = jnp.maximum(top, c)
    m_new = jnp.broadcast_to(jnp.max(top, axis=1, keepdims=True) * SCALE, top.shape)
    if carry is not None:
        m_new = jnp.maximum(carry[0], m_new)
    total = None
    rounded = []
    for c in chunks:
        w = jnp.exp2(c * SCALE - m_new)
        total = w if total is None else total + w
        rounded.append(w.astype(jnp.bfloat16))
    out = jnp.dot(jnp.concatenate(rounded, axis=1), v, preferred_element_type=jnp.float32)
    if carry is not None:
        alpha = jnp.exp2(carry[0] - m_new)
        total = carry[1] * alpha + total
        out = carry[2] * alpha + out
    return m_new, total, out


def fold_heads(q_ref, slot, kv_local, keys, values, bias, load, store):
    group, tree = q_ref.shape[1] // kv_local, q_ref.shape[2]
    rows = group * tree

    def scores_of(h):
        q = q_ref[slot, h * group : (h + 1) * group].reshape(rows, HD)
        return [dot_nt(q, k(h)) for k in keys]

    def values_of(h):
        parts = [v(h) for v in values]
        return parts[0] if len(parts) == 1 else jnp.concatenate(parts, axis=0)

    ahead = scores_of(0)
    for h in range(kv_local):
        now = ahead
        if h + 1 < kv_local:
            ahead = scores_of(h + 1)
        store(h, absorb(load(h), now, bias, values_of(h)))


def state_access(refs, r):
    def load(h):
        return tuple(ref[r, h] for ref in refs)

    def store(h, state):
        for ref, value in zip(refs, state):
            ref[r, h] = value

    return load, store


def fold_shards(q_ref, r, offset, kv_local, used, bases, base0, held, groups, states):
    n = held.shape[0] // 2
    count = held.shape[1]
    load, store = state_access(states, r)
    for group in groups:
        visible = [used - bases[base0 + i] for i in group]
        most = visible[0]
        for other in visible[1:]:
            most = jnp.maximum(most, other)

        @pl.when(most > 0)
        def _():
            slots = lax.broadcasted_iota(jnp.int32, (1, count), 1)
            fold_heads(
                q_ref,
                offset + r,
                kv_local,
                [lambda h, i=i: held[i, :, head_cols(h)] for i in group],
                [lambda h, i=i: held[n + i, :, head_cols(h)] for i in group],
                [jnp.where(slots < v, 0.0, NEG_FILL) for v in visible],
                load,
                store,
            )


def pairs_of(n):
    return [tuple(range(i, min(i + 2, n))) for i in range(0, n, 2)]


def first_kernel(kv_local, near, block, n_shards, offset, base0, info, bases, q_ref, kn_ref, vn_ref, anc_ref, ck_ref, cv_ref, *refs):
    sources = refs[: 2 * n_shards]
    m_out, l_out, acc_out, k_near, v_near, held, sems = refs[-7:]
    states = (m_out, l_out, acc_out)
    copies = fetch_all(sources, held, sems)
    reqs = m_out.shape[0]
    n_heads, tree = q_ref.shape[1:3]
    group = n_heads // kv_local
    capacity = ck_ref.shape[0]
    for copy in copies:
        copy.wait()
    for r in range(reqs):
        load, store = state_access(states, r)
        low = info[0, offset + r]
        high = info[1, offset + r]
        start0 = pl.multiple_of(jnp.minimum((low // 16) * 16, capacity - near), 16)
        k_near[0:tree] = kn_ref[(offset + r) * tree : (offset + r + 1) * tree]
        v_near[0:tree] = vn_ref[(offset + r) * tree : (offset + r + 1) * tree]
        k_near[tree : tree + near] = ck_ref[pl.ds(start0, near), :]
        v_near[tree : tree + near] = cv_ref[pl.ds(start0, near), :]
        column = lax.broadcasted_iota(jnp.int32, (tree, tree + near), 1)
        slots = column - tree + start0
        seen = ((slots >= low) & (slots < high)).astype(jnp.float32)
        linked = jnp.concatenate([anc_ref[offset + r], jnp.zeros((tree, tree + near - HD), jnp.float32)], axis=1)
        bias = jnp.where(jnp.where(column < tree, linked, seen) > 0.5, 0.0, NEG_FILL)
        bias = jnp.concatenate([bias] * group, axis=0)
        seen = [info[2, offset + r] - bases[base0 + i] for i in range(n_shards)]
        place = lax.broadcasted_iota(jnp.int32, (1, held.shape[1]), 1)
        fold_heads(
            q_ref,
            offset + r,
            kv_local,
            [lambda h: k_near[:, head_cols(h)]] + [lambda h, i=i: held[i, :, head_cols(h)] for i in range(n_shards)],
            [lambda h: v_near[:, head_cols(h)]]
            + [lambda h, i=i: held[n_shards + i, :, head_cols(h)] for i in range(n_shards)],
            [bias] + [jnp.where(place < count, 0.0, NEG_FILL) for count in seen],
            lambda h: None,
            store,
        )
        begin0 = start0 + near

        def step(i, _):
            begin = begin0 + i * block
            start = pl.multiple_of(jnp.minimum(begin, capacity - block), 16)
            place = start + lax.broadcasted_iota(jnp.int32, (1, block), 1)
            mask = jnp.where((place >= begin) & (place < high), 0.0, NEG_FILL)
            fold_heads(
                q_ref,
                offset + r,
                kv_local,
                [lambda h: ck_ref[pl.ds(start, block), head_cols(h)]],
                [lambda h: cv_ref[pl.ds(start, block), head_cols(h)]],
                [mask],
                load,
                store,
            )
            return 0

        lax.fori_loop(0, (jnp.maximum(high - begin0, 0) + block - 1) // block, step, 0)


def state_shapes(reqs, kv_local, rows):
    return [jax.ShapeDtypeStruct((reqs, kv_local, rows, HD), jnp.float32)] * 3


def shard_scratch(shards):
    n = 2 * len(shards)
    return [pltpu.VMEM((n,) + shards[0][0].shape, jnp.bfloat16), pltpu.SemaphoreType.DMA((n,))]


def flat(shards):
    return [k for k, _ in shards] + [v for _, v in shards]


def attend_first(parts, ancestry, cache_keys, cache_values, info, bases, shards, span, offset, reqs, after=()):
    queries, new_keys, new_values = parts
    shards = shards[span[0] : span[1]]
    _, n_heads, tree, _ = queries.shape
    capacity, cols = cache_keys.shape
    kv_local = cols // HD
    near = min(384 - tree, capacity)
    block = min(1792, capacity)
    n = len(shards)
    return call(
        functools.partial(first_kernel, kv_local, near, block, n, offset, span[0]),
        [SMEM] * 2 + [VMEM] * 6 + [HBM] * (2 * n),
        [info, bases, queries, new_keys, new_values, ancestry, cache_keys, cache_values, *flat(shards)],
        state_shapes(reqs, kv_local, n_heads // kv_local * tree),
        [pltpu.VMEM((tree + near, cols), jnp.bfloat16)] * 2 + shard_scratch(shards),
        40,
        6,
        "attend_first",
        after,
    )


def middle_kernel(kv_local, n_shards, offset, groups, base0, info, bases, q_ref, *refs):
    sources = refs[: 2 * n_shards]
    ins = refs[2 * n_shards : 2 * n_shards + 3]
    outs = refs[2 * n_shards + 3 : 2 * n_shards + 6]
    held, sems = refs[2 * n_shards + 6 :]
    copies = fetch_all(sources, held, sems)
    reqs = outs[0].shape[0]
    for src, dst in zip(ins, outs):
        dst[...] = src[offset : offset + reqs]
    for copy in copies:
        copy.wait()
    for r in range(reqs):
        fold_shards(q_ref, r, offset, kv_local, info[2, offset + r], bases, base0, held, groups, outs)


def attend_middle(queries, info, bases, shards, span, state, offset, reqs):
    shards = shards[span[0] : span[1]]
    _, n_heads, tree, _ = queries.shape
    kv_local = shards[0][0].shape[1] // HD
    n = len(shards)
    return call(
        functools.partial(middle_kernel, kv_local, n, offset, pairs_of(n), span[0]),
        [SMEM] * 2 + [VMEM] + [HBM] * (2 * n) + [VMEM] * 3,
        [info, bases, queries, *flat(shards), *state],
        state_shapes(reqs, kv_local, n_heads // kv_local * tree),
        shard_scratch(shards),
        40,
        0.3 + 0.2 * n * reqs,
        "attend_middle",
    )


def last_kernel(kv_local, n_shards, offset, groups, base0, block, info, bases, q_ref, *refs):
    sources = refs[: 2 * n_shards]
    ins = refs[2 * n_shards : 2 * n_shards + 3]
    w_ref = refs[2 * n_shards + 3]
    m_s, l_s, acc_s, attended, w_held, w_sems, held, sems = refs[-8:]
    reqs = m_s.shape[0]
    n_heads, tree = q_ref.shape[1:3]
    outs = refs[-8 - reqs : -8]
    states = (m_s, l_s, acc_s)
    group = n_heads // kv_local
    copies = fetch_all(sources, held, sems)
    cuts = [slice(lo, lo + block) for lo in range(0, w_ref.shape[1], block)]
    w_copies = fetch_all([w_ref.at[:, cut] for cut in cuts], w_held, w_sems)
    for src, dst in zip(ins, states):
        lead = 0 if src.shape[0] == reqs else offset
        dst[...] = src[lead : lead + reqs]
    for copy in copies:
        copy.wait()
    for r in range(reqs):
        fold_shards(q_ref, r, offset, kv_local, info[2, offset + r], bases, base0, held, groups, states)
        for h in range(kv_local):
            total = jnp.sum(l_s[r, h], axis=1, keepdims=True)
            result = (acc_s[r, h] / total).astype(jnp.bfloat16)
            for g in range(group):
                attended[r, :, head_cols(h * group + g)] = result[g * tree : (g + 1) * tree]
    x = attended[...].reshape(reqs * tree, n_heads * HD)
    for i, cut in enumerate(cuts):
        w_copies[i].wait()
        product = jnp.dot(x, w_held[i], preferred_element_type=jnp.float32).astype(jnp.bfloat16)
        for r in range(reqs):
            outs[r][:, cut] = product[r * tree : (r + 1) * tree]


def attend_last(queries, info, bases, shards, span, state, w_out, offset, reqs, after=()):
    shards = shards[span[0] : span[1]]
    _, n_heads, tree, _ = queries.shape
    kv_local = shards[0][0].shape[1] // HD
    rows = n_heads // kv_local * tree
    n = len(shards)
    depth, width = w_out.shape
    block = min(1024, width)
    return call(
        functools.partial(last_kernel, kv_local, n, offset, pairs_of(n), span[0], block),
        [SMEM] * 2 + [VMEM] + [HBM] * (2 * n) + [VMEM] * 3 + [HBM],
        [info, bases, queries, *flat(shards), *state, w_out],
        [jax.ShapeDtypeStruct((tree, width), jnp.bfloat16)] * reqs,
        [pltpu.VMEM((reqs, kv_local, rows, HD), jnp.float32)] * 3
        + [
            pltpu.VMEM((reqs, tree, n_heads * HD), jnp.bfloat16),
            pltpu.VMEM((width // block, depth, block), jnp.bfloat16),
            pltpu.SemaphoreType.DMA((width // block,)),
        ]
        + shard_scratch(shards),
        50,
        3.5 + 0.4 * n * reqs,
        "attend_last",
        after,
    )


def add_kernel(*refs):
    total = refs[0][...].astype(jnp.float32)
    for ref in refs[1:-1]:
        total = total + ref[...].astype(jnp.float32)
    refs[-1][...] = total.astype(refs[-1].dtype)


def add_up(*terms, dtype=jnp.bfloat16):
    outs = call(
        add_kernel,
        [VMEM] * len(terms),
        list(terms),
        [jax.ShapeDtypeStruct(terms[0].shape, dtype)],
        [],
        8,
        1,
        "add_up",
    )
    return outs[0]


def ancestor_table(parents):
    node_count = parents.shape[-1]
    column = jnp.arange(node_count, dtype=jnp.int32)
    linked = (parents[..., None] == column) | (column[:, None] == column[None, :])
    ancestry = linked.astype(jnp.bfloat16)
    for repeat in range((node_count - 1).bit_length()):
        paths = jnp.einsum("rij,rjk->rik", ancestry, ancestry, preferred_element_type=jnp.float32)
        ancestry = jnp.minimum(paths, 1.0).astype(jnp.bfloat16)
    return ancestry.astype(jnp.float32)


def rotary_tables(position):
    half = HD // 2
    frequency = 10000.0 ** (-jnp.arange(half, dtype=jnp.float32) / half)
    angles = position.astype(jnp.float32)[:, None] * frequency[None, :]
    cosine = jnp.cos(angles)
    sine = jnp.sin(angles)
    return jnp.concatenate([cosine, cosine], axis=1), jnp.concatenate([-sine, sine], axis=1)


def swap_pairs(batch, tensor, move):
    columns = 2
    pairs = []
    for z in range(batch // columns):
        for x in range(columns):
            for t in range(tensor):
                z2, x2, t2 = move(z, x, t)
                pairs.append(((z * columns + x) * tensor + t, (z2 * columns + x2) * tensor + t2))
    return pairs


def body(
    sizes,
    tokens,
    norm_gain,
    w_query,
    w_key,
    w_value,
    w_out,
    prefix_keys,
    prefix_values,
    cache_keys,
    cache_values,
    cache_lengths,
    prefix_used,
    parents,
    accepted_index,
):
    batch, tensor = sizes
    reqs, tree = parents.shape
    shard_rows = prefix_keys.shape[0]
    fast = sizes == (8, 4) and reqs == tensor and tokens.shape[0] == tree
    me_batch = lax.axis_index("batch")
    me_tensor = lax.axis_index("tensor")
    slots = jnp.arange(reqs, dtype=jnp.int32)

    if fast:
        pairs = functools.partial(swap_pairs, batch, tensor)
        core_pairs = pairs(lambda z, x, t: (z, x, t ^ 1))
        y_pairs = pairs(lambda z, x, t: (z, x, t ^ 2))
        x_pairs = pairs(lambda z, x, t: (z, 1 - x, t))
        z_pairs = pairs(lambda z, x, t: ((z + 1) % (batch // 2), x, t))
        send = lambda a, p: lax.ppermute(a, AXES, p)
        core_tokens = send(tokens, core_pairs)
        y_tokens = send(tokens, y_pairs)
        far_tokens = send(y_tokens, core_pairs)
    order = slots ^ me_tensor if fast else slots
    pick = order[:, None] == slots[None, :]
    own_lengths = lax.dynamic_slice_in_dim(cache_lengths, me_batch * reqs, reqs)
    lower = jnp.cumsum(own_lengths) - own_lengths
    table = jnp.stack([lower, lower + own_lengths, prefix_used])
    info = jnp.sum(jnp.where(pick[None], table[:, None, :], 0), axis=2)
    tree_parents = jnp.sum(jnp.where(pick[:, :, None], parents[None], 0), axis=1)
    ancestry = ancestor_table(tree_parents)
    tree_depth = (jnp.sum(ancestry, axis=-1) - 1.0).astype(jnp.int32)
    position = ((info[2] + info[1] - info[0])[:, None] + tree_depth).reshape(reqs * tree)
    if fast:
        steps = batch // 2
        own_keys, own_values, _ = lax.optimization_barrier((prefix_keys, prefix_values, own_lengths))
        ring = [(prefix_keys, prefix_values)]
        ring.append((send(own_keys, z_pairs), send(own_values, z_pairs)))
        side = [(send(own_keys, x_pairs), send(own_values, x_pairs))]
    cosine, sine = rotary_tables(position)
    ancestry = jnp.pad(ancestry, ((0, 0), (0, 0), (0, HD - tree)))
    shard_ids = jnp.arange(batch, dtype=jnp.int32)
    if fast:
        z, x = me_batch // 2, me_batch % 2
        shard_ids = (z - shard_ids // 2) % (batch // 2) * 2 + (x ^ (shard_ids % 2))
    bases = (shard_ids * shard_rows).astype(jnp.int32)

    def projected(token_list, after=()):
        return project(token_list, norm_gain[None, :], cosine, sine, w_query, w_key, w_value, tree, after)

    if fast:
        def pass_on(step, after):
            keys, values, _ = lax.optimization_barrier((*ring[step], after))
            if step < steps - 1:
                ring.append((send(keys, z_pairs), send(values, z_pairs)))
                side.append((send(keys, x_pairs), send(values, x_pairs)))
            else:
                side.append((send(keys, x_pairs), send(side[-1][1], z_pairs)))

        pass_on(1, cosine)
        parts = projected([tokens, core_tokens, y_tokens, far_tokens])
        queries, new_keys, new_values = parts
        pass_on(2, queries)
        shards = [shard for s in range(steps - 1) for shard in (ring[s], side[s])]
        first = functools.partial(
            attend_first,
            (queries, new_keys, new_values),
            ancestry,
            cache_keys,
            cache_values,
            info,
            bases,
            shards,
            (0, 2),
            reqs=reqs,
        )
        state = first(offset=0)
        pass_on(steps - 1, state[0])
        shards += [ring[-1], side[-1]]
        n = len(shards)
        state = attend_middle(queries, info, bases, shards, (2, 5), state, 0, reqs)
        far_state = attend_middle(queries, info, bases, shards, (5, n - 1), state, 2, 2)
        final = functools.partial(attend_last, queries, info, bases, shards, w_out=w_out, reqs=2)
        kept, away = final((n - 1, n), far_state, offset=2)
        got = send(away, core_pairs)
        summed = add_up(kept, got)
        far = send(summed, y_pairs)
        kept, away = final((5, n), state, offset=0, after=(summed,))
        got = send(away, core_pairs)
        mixed_rows = add_up(add_up(kept, far, dtype=jnp.float32), got)
    else:
        gathered = lax.all_gather(tokens, "tensor", axis=0, tiled=True)
        parts = projected([gathered])
        queries, new_keys, new_values = parts
        all_keys = lax.all_gather(prefix_keys, "batch", axis=0, tiled=True)
        all_values = lax.all_gather(prefix_values, "batch", axis=0, tiled=True)
        split = lambda a: [a[i * shard_rows : (i + 1) * shard_rows] for i in range(batch)]
        shards = list(zip(split(all_keys), split(all_values)))
        state = attend_first(parts, ancestry, cache_keys, cache_values, info, bases, shards, (0, 2), 0, reqs)
        for s in range(2, batch - 2, 4):
            state = attend_middle(queries, info, bases, shards, (s, min(s + 4, batch - 2)), state, 0, reqs)
        partial = attend_last(queries, info, bases, shards, (batch - 2, batch), state, w_out, 0, reqs)
        mixed_rows = lax.psum_scatter(
            jnp.concatenate(partial, axis=0), "tensor", scatter_dimension=0, tiled=True
        )
    rows = ((slots ^ me_tensor if fast else slots)[:, None] * tree + accepted_index).reshape(-1)
    accepted_keys = jnp.take(new_keys, rows, axis=0).reshape(reqs, accepted_index.shape[1], -1)
    accepted_values = jnp.take(new_values, rows, axis=0).reshape(reqs, accepted_index.shape[1], -1)
    return (mixed_rows, accepted_keys, accepted_values)


def solution(mesh):
    sizes = (mesh.shape["batch"], mesh.shape["tensor"])
    in_specs = (
        P(("batch", "tensor"), None),
        P(),
        P(None, "tensor"),
        P(None, "tensor"),
        P(None, "tensor"),
        P("tensor", None),
        P("batch", "tensor"),
        P("batch", "tensor"),
        P("batch", "tensor"),
        P("batch", "tensor"),
        P(),
        P("batch"),
        P("batch", None),
        P("batch", None),
    )
    out_specs = (
        P(("batch", "tensor"), None),
        P("batch", None, "tensor"),
        P("batch", None, "tensor"),
    )
    return jax.shard_map(
        functools.partial(body, sizes), mesh=mesh, in_specs=in_specs, out_specs=out_specs, check_vma=False
    )
```

```python
import functools

import jax
import jax.numpy as jnp
from jax import lax
from jax.experimental import pallas as pl
from jax.experimental.pallas import tpu as pltpu
from jax.sharding import PartitionSpec as P

HD = 128
NEG_FILL = -1e30
LOG2E = 1.4426950408889634
AXES = ("batch", "tensor")
SCALE = HD**-0.5 * LOG2E
COST = 1.1e9
HBM = pl.BlockSpec(memory_space=pltpu.HBM)
VMEM = pl.BlockSpec(memory_space=pltpu.VMEM)
SMEM = pl.BlockSpec(memory_space=pltpu.SMEM)


def call(kernel, in_specs, args, out_shape, scratch, megabytes, microseconds, name, after=()):
    n_in, n_out = len(args), len(out_shape)

    def wrapped(*refs):
        kernel(*refs[:n_in], *refs[n_in + len(after) :])

    return pl.pallas_call(
        wrapped,
        in_specs=in_specs + [HBM] * len(after),
        out_specs=[VMEM] * n_out,
        out_shape=out_shape,
        scratch_shapes=scratch,
        compiler_params=pltpu.CompilerParams(vmem_limit_bytes=megabytes * 2**20),
        cost_estimate=pl.CostEstimate(flops=int(microseconds * COST), bytes_accessed=0, transcendentals=0),
        name=name,
    )(*args, *after)


def dot_nt(a, b):
    return lax.dot_general(a, b, (((1,), (1,)), ((), ())), preferred_element_type=jnp.float32)


def head_cols(h):
    return slice(h * HD, (h + 1) * HD)


def fetch_all(sources, held, sems):
    copies = [pltpu.make_async_copy(src, held.at[i], sems.at[i]) for i, src in enumerate(sources)]
    for copy in copies:
        copy.start()
    return copies


def qkv_kernel(n_tok, n_heads, kv_local, steps, *refs):
    token_refs = refs[:n_tok]
    gain_ref, cos_ref, sin_ref = refs[n_tok : n_tok + 3]
    weights = refs[n_tok + 3 : n_tok + 6]
    q_out, k_out, v_out, held, normed, acc, wq, wk, wv, sems, weight_sems = refs[n_tok + 6 :]
    copies = fetch_all(token_refs, held, sems)
    depth = wq.shape[0] // steps
    chunks = []
    for s in range(steps):
        span = slice(s * depth, (s + 1) * depth)
        chunks.append(
            [
                pltpu.make_async_copy(src.at[span], dst.at[span], weight_sems.at[s, i])
                for i, (src, dst) in enumerate(zip(weights, (wq, wk, wv)))
            ]
        )
        for copy in chunks[-1]:
            copy.start()
    rows = held.shape[1]
    step = min(16, rows)
    for i in range(n_tok):
        copies[i].wait()
        for lo in range(0, rows, step):
            values = held[i, lo : lo + step].astype(jnp.float32)
            factor = lax.rsqrt(jnp.mean(values * values, axis=-1, keepdims=True) + 1e-05)
            normed[i * rows + lo : i * rows + lo + step] = (values * factor * gain_ref[...]).astype(jnp.bfloat16)
    cosine = cos_ref[...]
    sine = sin_ref[...]
    reqs, tree = q_out.shape[0], q_out.shape[2]

    def rotated(raw):
        return (raw * cosine + pltpu.roll(raw, HD // 2, 1) * sine).astype(jnp.bfloat16)

    for s in range(steps):
        for copy in chunks[s]:
            copy.wait()
        span = slice(s * depth, (s + 1) * depth)
        x = normed[:, span]
        lo = 0
        for which, w in enumerate((wq, wk, wv)):
            width = w.shape[1]
            raw = jnp.dot(x, w[span], preferred_element_type=jnp.float32)
            if s > 0:
                raw = acc[:, lo : lo + width] + raw
            if s < steps - 1:
                acc[:, lo : lo + width] = raw
            elif which == 0:
                for head in range(n_heads):
                    out = rotated(raw[:, head_cols(head)])
                    for r in range(reqs):
                        q_out[r, head] = out[r * tree : (r + 1) * tree]
            elif which == 1:
                for head in range(kv_local):
                    k_out[:, head_cols(head)] = rotated(raw[:, head_cols(head)])
            else:
                v_out[...] = raw.astype(jnp.bfloat16)
            lo += width


def project(token_list, gain, cosine, sine, w_query, w_key, w_value, tree, after=()):
    rows, width = token_list[0].shape
    n_tok = len(token_list)
    total = rows * n_tok
    n_heads = w_query.shape[1] // HD
    cols = w_key.shape[1]
    steps = 4
    return call(
        functools.partial(qkv_kernel, n_tok, n_heads, cols // HD, steps),
        [HBM] * n_tok + [VMEM] * 3 + [HBM] * 3,
        [*token_list, gain, cosine, sine, w_query, w_key, w_value],
        [
            jax.ShapeDtypeStruct((total // tree, n_heads, tree, HD), jnp.bfloat16),
            jax.ShapeDtypeStruct((total, cols), jnp.bfloat16),
            jax.ShapeDtypeStruct((total, cols), jnp.bfloat16),
        ],
        [
            pltpu.VMEM((n_tok, rows, width), jnp.bfloat16),
            pltpu.VMEM((total, width), jnp.bfloat16),
            pltpu.VMEM((total, w_query.shape[1] + 2 * cols), jnp.float32),
            pltpu.VMEM(w_query.shape, jnp.bfloat16),
            pltpu.VMEM(w_key.shape, jnp.bfloat16),
            pltpu.VMEM(w_value.shape, jnp.bfloat16),
            pltpu.SemaphoreType.DMA((n_tok,)),
            pltpu.SemaphoreType.DMA((steps, 3)),
        ],
        50,
        7,
        "project",
        after,
    )


def absorb(carry, scores, biases, v):
    chunks = []
    for s, bias in zip(scores, biases):
        s = s + bias
        chunks += [s[:, j : j + HD] for j in range(0, s.shape[1], HD)]
    top = chunks[0]
    for c in chunks[1:]:
        top = jnp.maximum(top, c)
    m_new = jnp.broadcast_to(jnp.max(top, axis=1, keepdims=True) * SCALE, top.shape)
    if carry is not None:
        m_new = jnp.maximum(carry[0], m_new)
    total = None
    rounded = []
    for c in chunks:
        w = jnp.exp2(c * SCALE - m_new)
        total = w if total is None else total + w
        rounded.append(w.astype(jnp.bfloat16))
    out = jnp.dot(jnp.concatenate(rounded, axis=1), v, preferred_element_type=jnp.float32)
    if carry is not None:
        alpha = jnp.exp2(carry[0] - m_new)
        total = carry[1] * alpha + total
        out = carry[2] * alpha + out
    return m_new, total, out


def fold_heads(q_ref, slot, kv_local, keys, values, bias, load, store):
    group, tree = q_ref.shape[1] // kv_local, q_ref.shape[2]
    rows = group * tree

    def scores_of(h):
        q = q_ref[slot, h * group : (h + 1) * group].reshape(rows, HD)
        return [dot_nt(q, k(h)) for k in keys]

    def values_of(h):
        parts = [v(h) for v in values]
        return parts[0] if len(parts) == 1 else jnp.concatenate(parts, axis=0)

    ahead = scores_of(0)
    for h in range(kv_local):
        now = ahead
        if h + 1 < kv_local:
            ahead = scores_of(h + 1)
        store(h, absorb(load(h), now, bias, values_of(h)))


def state_access(refs, r):
    def load(h):
        return tuple(ref[r, h] for ref in refs)

    def store(h, state):
        for ref, value in zip(refs, state):
            ref[r, h] = value

    return load, store


def fold_shards(q_ref, r, offset, kv_local, used, bases, base0, held, groups, states):
    n = held.shape[0] // 2
    count = held.shape[1]
    load, store = state_access(states, r)
    for group in groups:
        visible = [used - bases[base0 + i] for i in group]
        most = visible[0]
        for other in visible[1:]:
            most = jnp.maximum(most, other)

        @pl.when(most > 0)
        def _():
            slots = lax.broadcasted_iota(jnp.int32, (1, count), 1)
            fold_heads(
                q_ref,
                offset + r,
                kv_local,
                [lambda h, i=i: held[i, :, head_cols(h)] for i in group],
                [lambda h, i=i: held[n + i, :, head_cols(h)] for i in group],
                [jnp.where(slots < v, 0.0, NEG_FILL) for v in visible],
                load,
                store,
            )


def pairs_of(n):
    return [tuple(range(i, min(i + 2, n))) for i in range(0, n, 2)]


def first_kernel(kv_local, near, block, n_shards, offset, base0, info, bases, q_ref, kn_ref, vn_ref, anc_ref, ck_ref, cv_ref, *refs):
    sources = refs[: 2 * n_shards]
    m_out, l_out, acc_out, k_near, v_near, held, sems = refs[-7:]
    states = (m_out, l_out, acc_out)
    copies = fetch_all(sources, held, sems)
    reqs = m_out.shape[0]
    n_heads, tree = q_ref.shape[1:3]
    group = n_heads // kv_local
    capacity = ck_ref.shape[0]
    for copy in copies:
        copy.wait()
    def one_request(r, _):
        load, store = state_access(states, r)
        low = info[0, offset + r]
        high = info[1, offset + r]
        start0 = pl.multiple_of(jnp.minimum((low // 16) * 16, capacity - near), 16)
        own_rows = pl.ds(pl.multiple_of((offset + r) * tree, tree), tree)
        k_near[0:tree] = kn_ref[own_rows, :]
        v_near[0:tree] = vn_ref[own_rows, :]
        k_near[tree : tree + near] = ck_ref[pl.ds(start0, near), :]
        v_near[tree : tree + near] = cv_ref[pl.ds(start0, near), :]
        column = lax.broadcasted_iota(jnp.int32, (tree, tree + near), 1)
        slots = column - tree + start0
        seen = ((slots >= low) & (slots < high)).astype(jnp.float32)
        linked = jnp.concatenate([anc_ref[offset + r], jnp.zeros((tree, tree + near - HD), jnp.float32)], axis=1)
        bias = jnp.where(jnp.where(column < tree, linked, seen) > 0.5, 0.0, NEG_FILL)
        bias = jnp.concatenate([bias] * group, axis=0)
        seen = [info[2, offset + r] - bases[base0 + i] for i in range(n_shards)]
        place = lax.broadcasted_iota(jnp.int32, (1, held.shape[1]), 1)
        fold_heads(
            q_ref,
            offset + r,
            kv_local,
            [lambda h: k_near[:, head_cols(h)]] + [lambda h, i=i: held[i, :, head_cols(h)] for i in range(n_shards)],
            [lambda h: v_near[:, head_cols(h)]]
            + [lambda h, i=i: held[n_shards + i, :, head_cols(h)] for i in range(n_shards)],
            [bias] + [jnp.where(place < count, 0.0, NEG_FILL) for count in seen],
            lambda h: None,
            store,
        )
        begin0 = start0 + near

        def step(i, _):
            begin = begin0 + i * block
            start = pl.multiple_of(jnp.minimum(begin, capacity - block), 16)
            place = start + lax.broadcasted_iota(jnp.int32, (1, block), 1)
            mask = jnp.where((place >= begin) & (place < high), 0.0, NEG_FILL)
            fold_heads(
                q_ref,
                offset + r,
                kv_local,
                [lambda h: ck_ref[pl.ds(start, block), head_cols(h)]],
                [lambda h: cv_ref[pl.ds(start, block), head_cols(h)]],
                [mask],
                load,
                store,
            )
            return 0

        lax.fori_loop(0, (jnp.maximum(high - begin0, 0) + block - 1) // block, step, 0)
        return 0

    lax.fori_loop(0, reqs, one_request, 0)


def state_shapes(reqs, kv_local, rows):
    return [jax.ShapeDtypeStruct((reqs, kv_local, rows, HD), jnp.float32)] * 3


def shard_scratch(shards):
    n = 2 * len(shards)
    return [pltpu.VMEM((n,) + shards[0][0].shape, jnp.bfloat16), pltpu.SemaphoreType.DMA((n,))]


def flat(shards):
    return [k for k, _ in shards] + [v for _, v in shards]


def attend_first(parts, ancestry, cache_keys, cache_values, info, bases, shards, span, offset, reqs, after=()):
    queries, new_keys, new_values = parts
    shards = shards[span[0] : span[1]]
    _, n_heads, tree, _ = queries.shape
    capacity, cols = cache_keys.shape
    kv_local = cols // HD
    near = min(384 - tree, capacity)
    block = min(1792, capacity)
    n = len(shards)
    return call(
        functools.partial(first_kernel, kv_local, near, block, n, offset, span[0]),
        [SMEM] * 2 + [VMEM] * 6 + [HBM] * (2 * n),
        [info, bases, queries, new_keys, new_values, ancestry, cache_keys, cache_values, *flat(shards)],
        state_shapes(reqs, kv_local, n_heads // kv_local * tree),
        [pltpu.VMEM((tree + near, cols), jnp.bfloat16)] * 2 + shard_scratch(shards),
        40,
        6,
        "attend_first",
        after,
    )


def middle_kernel(kv_local, n_shards, offset, groups, base0, info, bases, q_ref, *refs):
    sources = refs[: 2 * n_shards]
    ins = refs[2 * n_shards : 2 * n_shards + 3]
    outs = refs[2 * n_shards + 3 : 2 * n_shards + 6]
    held, sems = refs[2 * n_shards + 6 :]
    copies = fetch_all(sources, held, sems)
    reqs = outs[0].shape[0]
    for src, dst in zip(ins, outs):
        dst[...] = src[offset : offset + reqs]
    for copy in copies:
        copy.wait()

    def one_request(r, _):
        fold_shards(q_ref, r, offset, kv_local, info[2, offset + r], bases, base0, held, groups, outs)
        return 0

    lax.fori_loop(0, reqs, one_request, 0)


def attend_middle(queries, info, bases, shards, span, state, offset, reqs):
    shards = shards[span[0] : span[1]]
    _, n_heads, tree, _ = queries.shape
    kv_local = shards[0][0].shape[1] // HD
    n = len(shards)
    return call(
        functools.partial(middle_kernel, kv_local, n, offset, pairs_of(n), span[0]),
        [SMEM] * 2 + [VMEM] + [HBM] * (2 * n) + [VMEM] * 3,
        [info, bases, queries, *flat(shards), *state],
        state_shapes(reqs, kv_local, n_heads // kv_local * tree),
        shard_scratch(shards),
        40,
        0.3 + 0.2 * n * reqs,
        "attend_middle",
    )


def last_kernel(kv_local, n_shards, offset, groups, base0, block, info, bases, q_ref, *refs):
    sources = refs[: 2 * n_shards]
    ins = refs[2 * n_shards : 2 * n_shards + 3]
    w_ref = refs[2 * n_shards + 3]
    m_s, l_s, acc_s, attended, w_held, w_sems, held, sems = refs[-8:]
    reqs = m_s.shape[0]
    n_heads, tree = q_ref.shape[1:3]
    outs = refs[-8 - reqs : -8]
    states = (m_s, l_s, acc_s)
    group = n_heads // kv_local
    copies = fetch_all(sources, held, sems)
    cuts = [slice(lo, lo + block) for lo in range(0, w_ref.shape[1], block)]
    w_copies = fetch_all([w_ref.at[:, cut] for cut in cuts], w_held, w_sems)
    for src, dst in zip(ins, states):
        lead = 0 if src.shape[0] == reqs else offset
        dst[...] = src[lead : lead + reqs]
    for copy in copies:
        copy.wait()

    def one_request(r, _):
        fold_shards(q_ref, r, offset, kv_local, info[2, offset + r], bases, base0, held, groups, states)
        for h in range(kv_local):
            total = jnp.sum(l_s[r, h], axis=1, keepdims=True)
            result = (acc_s[r, h] / total).astype(jnp.bfloat16)
            for g in range(group):
                attended[r, :, head_cols(h * group + g)] = result[g * tree : (g + 1) * tree]
        return 0

    lax.fori_loop(0, reqs, one_request, 0)
    x = attended[...].reshape(reqs * tree, n_heads * HD)
    for i, cut in enumerate(cuts):
        w_copies[i].wait()
        product = jnp.dot(x, w_held[i], preferred_element_type=jnp.float32).astype(jnp.bfloat16)
        for r in range(reqs):
            outs[r][:, cut] = product[r * tree : (r + 1) * tree]


def attend_last(queries, info, bases, shards, span, state, w_out, offset, reqs, after=()):
    shards = shards[span[0] : span[1]]
    _, n_heads, tree, _ = queries.shape
    kv_local = shards[0][0].shape[1] // HD
    rows = n_heads // kv_local * tree
    n = len(shards)
    depth, width = w_out.shape
    block = min(1024, width)
    return call(
        functools.partial(last_kernel, kv_local, n, offset, pairs_of(n), span[0], block),
        [SMEM] * 2 + [VMEM] + [HBM] * (2 * n) + [VMEM] * 3 + [HBM],
        [info, bases, queries, *flat(shards), *state, w_out],
        [jax.ShapeDtypeStruct((tree, width), jnp.bfloat16)] * reqs,
        [pltpu.VMEM((reqs, kv_local, rows, HD), jnp.float32)] * 3
        + [
            pltpu.VMEM((reqs, tree, n_heads * HD), jnp.bfloat16),
            pltpu.VMEM((width // block, depth, block), jnp.bfloat16),
            pltpu.SemaphoreType.DMA((width // block,)),
        ]
        + shard_scratch(shards),
        50,
        3.5 + 0.4 * n * reqs,
        "attend_last",
        after,
    )


def add_kernel(*refs):
    total = refs[0][...].astype(jnp.float32)
    for ref in refs[1:-1]:
        total = total + ref[...].astype(jnp.float32)
    refs[-1][...] = total.astype(refs[-1].dtype)


def add_up(*terms, dtype=jnp.bfloat16):
    outs = call(
        add_kernel,
        [VMEM] * len(terms),
        list(terms),
        [jax.ShapeDtypeStruct(terms[0].shape, dtype)],
        [],
        8,
        1,
        "add_up",
    )
    return outs[0]


def ancestor_table(parents):
    node_count = parents.shape[-1]
    column = jnp.arange(node_count, dtype=jnp.int32)
    linked = (parents[..., None] == column) | (column[:, None] == column[None, :])
    ancestry = linked.astype(jnp.bfloat16)
    for repeat in range((node_count - 1).bit_length()):
        paths = jnp.einsum("rij,rjk->rik", ancestry, ancestry, preferred_element_type=jnp.float32)
        ancestry = jnp.minimum(paths, 1.0).astype(jnp.bfloat16)
    return ancestry.astype(jnp.float32)


def rotary_tables(position):
    half = HD // 2
    frequency = 10000.0 ** (-jnp.arange(half, dtype=jnp.float32) / half)
    angles = position.astype(jnp.float32)[:, None] * frequency[None, :]
    cosine = jnp.cos(angles)
    sine = jnp.sin(angles)
    return jnp.concatenate([cosine, cosine], axis=1), jnp.concatenate([-sine, sine], axis=1)


def swap_pairs(batch, tensor, move):
    columns = 2
    pairs = []
    for z in range(batch // columns):
        for x in range(columns):
            for t in range(tensor):
                z2, x2, t2 = move(z, x, t)
                pairs.append(((z * columns + x) * tensor + t, (z2 * columns + x2) * tensor + t2))
    return pairs


def body(
    sizes,
    tokens,
    norm_gain,
    w_query,
    w_key,
    w_value,
    w_out,
    prefix_keys,
    prefix_values,
    cache_keys,
    cache_values,
    cache_lengths,
    prefix_used,
    parents,
    accepted_index,
):
    batch, tensor = sizes
    reqs, tree = parents.shape
    shard_rows = prefix_keys.shape[0]
    fast = sizes == (8, 4) and reqs == tensor and tokens.shape[0] == tree
    me_batch = lax.axis_index("batch")
    me_tensor = lax.axis_index("tensor")
    slots = jnp.arange(reqs, dtype=jnp.int32)

    if fast:
        pairs = functools.partial(swap_pairs, batch, tensor)
        core_pairs = pairs(lambda z, x, t: (z, x, t ^ 1))
        y_pairs = pairs(lambda z, x, t: (z, x, t ^ 2))
        x_pairs = pairs(lambda z, x, t: (z, 1 - x, t))
        z_pairs = pairs(lambda z, x, t: ((z + 1) % (batch // 2), x, t))
        send = lambda a, p: lax.ppermute(a, AXES, p)
        core_tokens = send(tokens, core_pairs)
        y_tokens = send(tokens, y_pairs)
        far_tokens = send(y_tokens, core_pairs)
    order = slots ^ me_tensor if fast else slots
    pick = order[:, None] == slots[None, :]
    own_lengths = lax.dynamic_slice_in_dim(cache_lengths, me_batch * reqs, reqs)
    lower = jnp.cumsum(own_lengths) - own_lengths
    table = jnp.stack([lower, lower + own_lengths, prefix_used])
    info = jnp.sum(jnp.where(pick[None], table[:, None, :], 0), axis=2)
    tree_parents = jnp.sum(jnp.where(pick[:, :, None], parents[None], 0), axis=1)
    ancestry = ancestor_table(tree_parents)
    tree_depth = (jnp.sum(ancestry, axis=-1) - 1.0).astype(jnp.int32)
    position = ((info[2] + info[1] - info[0])[:, None] + tree_depth).reshape(reqs * tree)
    if fast:
        steps = batch // 2
        own_keys, own_values, _ = lax.optimization_barrier((prefix_keys, prefix_values, own_lengths))
        ring = [(prefix_keys, prefix_values)]
        ring.append((send(own_keys, z_pairs), send(own_values, z_pairs)))
        side = [(send(own_keys, x_pairs), send(own_values, x_pairs))]
    cosine, sine = rotary_tables(position)
    ancestry = jnp.pad(ancestry, ((0, 0), (0, 0), (0, HD - tree)))
    shard_ids = jnp.arange(batch, dtype=jnp.int32)
    if fast:
        z, x = me_batch // 2, me_batch % 2
        shard_ids = (z - shard_ids // 2) % (batch // 2) * 2 + (x ^ (shard_ids % 2))
    bases = (shard_ids * shard_rows).astype(jnp.int32)

    def projected(token_list, after=()):
        return project(token_list, norm_gain[None, :], cosine, sine, w_query, w_key, w_value, tree, after)

    if fast:
        def pass_on(step, after):
            keys, values, _ = lax.optimization_barrier((*ring[step], after))
            if step < steps - 1:
                ring.append((send(keys, z_pairs), send(values, z_pairs)))
                side.append((send(keys, x_pairs), send(values, x_pairs)))
            else:
                side.append((send(keys, x_pairs), send(side[-1][1], z_pairs)))

        pass_on(1, cosine)
        parts = projected([tokens, core_tokens, y_tokens, far_tokens])
        queries, new_keys, new_values = parts
        pass_on(2, queries)
        shards = [shard for s in range(steps - 1) for shard in (ring[s], side[s])]
        first = functools.partial(
            attend_first,
            (queries, new_keys, new_values),
            ancestry,
            cache_keys,
            cache_values,
            info,
            bases,
            shards,
            (0, 2),
            reqs=reqs,
        )
        state = first(offset=0)
        pass_on(steps - 1, state[0])
        shards += [ring[-1], side[-1]]
        n = len(shards)
        state = attend_middle(queries, info, bases, shards, (2, 5), state, 0, reqs)
        far_state = attend_middle(queries, info, bases, shards, (5, n - 1), state, 2, 2)
        final = functools.partial(attend_last, queries, info, bases, shards, w_out=w_out, reqs=2)
        kept, away = final((n - 1, n), far_state, offset=2)
        got = send(away, core_pairs)
        summed = add_up(kept, got)
        far = send(summed, y_pairs)
        kept, away = final((5, n), state, offset=0, after=(summed,))
        got = send(away, core_pairs)
        mixed_rows = add_up(add_up(kept, far, dtype=jnp.float32), got)
    else:
        gathered = lax.all_gather(tokens, "tensor", axis=0, tiled=True)
        parts = projected([gathered])
        queries, new_keys, new_values = parts
        all_keys = lax.all_gather(prefix_keys, "batch", axis=0, tiled=True)
        all_values = lax.all_gather(prefix_values, "batch", axis=0, tiled=True)
        split = lambda a: [a[i * shard_rows : (i + 1) * shard_rows] for i in range(batch)]
        shards = list(zip(split(all_keys), split(all_values)))
        state = attend_first(parts, ancestry, cache_keys, cache_values, info, bases, shards, (0, 2), 0, reqs)
        for s in range(2, batch - 2, 4):
            state = attend_middle(queries, info, bases, shards, (s, min(s + 4, batch - 2)), state, 0, reqs)
        partial = attend_last(queries, info, bases, shards, (batch - 2, batch), state, w_out, 0, reqs)
        mixed_rows = lax.psum_scatter(
            jnp.concatenate(partial, axis=0), "tensor", scatter_dimension=0, tiled=True
        )
    rows = ((slots ^ me_tensor if fast else slots)[:, None] * tree + accepted_index).reshape(-1)
    accepted_keys = jnp.take(new_keys, rows, axis=0).reshape(reqs, accepted_index.shape[1], -1)
    accepted_values = jnp.take(new_values, rows, axis=0).reshape(reqs, accepted_index.shape[1], -1)
    return (mixed_rows, accepted_keys, accepted_values)


def solution(mesh):
    sizes = (mesh.shape["batch"], mesh.shape["tensor"])
    in_specs = (
        P(("batch", "tensor"), None),
        P(),
        P(None, "tensor"),
        P(None, "tensor"),
        P(None, "tensor"),
        P("tensor", None),
        P("batch", "tensor"),
        P("batch", "tensor"),
        P("batch", "tensor"),
        P("batch", "tensor"),
        P(),
        P("batch"),
        P("batch", None),
        P("batch", None),
    )
    out_specs = (
        P(("batch", "tensor"), None),
        P("batch", None, "tensor"),
        P("batch", None, "tensor"),
    )
    return jax.shard_map(
        functools.partial(body, sizes), mesh=mesh, in_specs=in_specs, out_specs=out_specs, check_vma=False
    )
```

```python
import functools

import jax
import jax.numpy as jnp
from jax import lax
from jax.experimental import pallas as pl
from jax.experimental.pallas import tpu as pltpu
from jax.sharding import PartitionSpec as P

HD = 128
NEG_FILL = -1e30
LOG2E = 1.4426950408889634
AXES = ("batch", "tensor")
SCALE = HD**-0.5 * LOG2E
COST = 1.1e9
HBM = pl.BlockSpec(memory_space=pltpu.HBM)
VMEM = pl.BlockSpec(memory_space=pltpu.VMEM)
SMEM = pl.BlockSpec(memory_space=pltpu.SMEM)


def call(kernel, in_specs, args, out_shape, scratch, megabytes, microseconds, name, after=()):
    n_in, n_out = len(args), len(out_shape)

    def wrapped(*refs):
        kernel(*refs[:n_in], *refs[n_in + len(after) :])

    return pl.pallas_call(
        wrapped,
        in_specs=in_specs + [HBM] * len(after),
        out_specs=[VMEM] * n_out,
        out_shape=out_shape,
        scratch_shapes=scratch,
        compiler_params=pltpu.CompilerParams(vmem_limit_bytes=megabytes * 2**20),
        cost_estimate=pl.CostEstimate(flops=int(microseconds * COST), bytes_accessed=0, transcendentals=0),
        name=name,
    )(*args, *after)


def dot_nt(a, b):
    return lax.dot_general(a, b, (((1,), (1,)), ((), ())), preferred_element_type=jnp.float32)


def head_cols(h):
    return slice(h * HD, (h + 1) * HD)


def fetch_all(sources, held, sems):
    copies = [pltpu.make_async_copy(src, held.at[i], sems.at[i]) for i, src in enumerate(sources)]
    for copy in copies:
        copy.start()
    return copies


def qkv_kernel(n_tok, n_heads, kv_local, steps, *refs):
    token_refs = refs[:n_tok]
    gain_ref, cos_ref, sin_ref = refs[n_tok : n_tok + 3]
    weights = refs[n_tok + 3 : n_tok + 6]
    q_out, k_out, v_out, held, normed, acc, wq, wk, wv, sems, weight_sems = refs[n_tok + 6 :]
    copies = fetch_all(token_refs, held, sems)
    depth = wq.shape[0] // steps
    chunks = []
    for s in range(steps):
        span = slice(s * depth, (s + 1) * depth)
        chunks.append(
            [
                pltpu.make_async_copy(src.at[span], dst.at[span], weight_sems.at[s, i])
                for i, (src, dst) in enumerate(zip(weights, (wq, wk, wv)))
            ]
        )
        for copy in chunks[-1]:
            copy.start()
    rows = held.shape[1]
    step = min(16, rows)
    for i in range(n_tok):
        copies[i].wait()
        for lo in range(0, rows, step):
            values = held[i, lo : lo + step].astype(jnp.float32)
            factor = lax.rsqrt(jnp.mean(values * values, axis=-1, keepdims=True) + 1e-05)
            normed[i * rows + lo : i * rows + lo + step] = (values * factor * gain_ref[...]).astype(jnp.bfloat16)
    cosine = cos_ref[...]
    sine = sin_ref[...]
    reqs, tree = q_out.shape[0], q_out.shape[2]

    def rotated(raw):
        return (raw * cosine + pltpu.roll(raw, HD // 2, 1) * sine).astype(jnp.bfloat16)

    for s in range(steps):
        for copy in chunks[s]:
            copy.wait()
        span = slice(s * depth, (s + 1) * depth)
        x = normed[:, span]
        lo = 0
        for which, w in enumerate((wq, wk, wv)):
            width = w.shape[1]
            raw = jnp.dot(x, w[span], preferred_element_type=jnp.float32)
            if s > 0:
                raw = acc[:, lo : lo + width] + raw
            if s < steps - 1:
                acc[:, lo : lo + width] = raw
            elif which == 0:
                for head in range(n_heads):
                    out = rotated(raw[:, head_cols(head)])
                    for r in range(reqs):
                        q_out[r, head] = out[r * tree : (r + 1) * tree]
            elif which == 1:
                for head in range(kv_local):
                    k_out[:, head_cols(head)] = rotated(raw[:, head_cols(head)])
            else:
                v_out[...] = raw.astype(jnp.bfloat16)
            lo += width


def project(token_list, gain, cosine, sine, w_query, w_key, w_value, tree, after=()):
    rows, width = token_list[0].shape
    n_tok = len(token_list)
    total = rows * n_tok
    n_heads = w_query.shape[1] // HD
    cols = w_key.shape[1]
    steps = 4
    return call(
        functools.partial(qkv_kernel, n_tok, n_heads, cols // HD, steps),
        [HBM] * n_tok + [VMEM] * 3 + [HBM] * 3,
        [*token_list, gain, cosine, sine, w_query, w_key, w_value],
        [
            jax.ShapeDtypeStruct((total // tree, n_heads, tree, HD), jnp.bfloat16),
            jax.ShapeDtypeStruct((total, cols), jnp.bfloat16),
            jax.ShapeDtypeStruct((total, cols), jnp.bfloat16),
        ],
        [
            pltpu.VMEM((n_tok, rows, width), jnp.bfloat16),
            pltpu.VMEM((total, width), jnp.bfloat16),
            pltpu.VMEM((total, w_query.shape[1] + 2 * cols), jnp.float32),
            pltpu.VMEM(w_query.shape, jnp.bfloat16),
            pltpu.VMEM(w_key.shape, jnp.bfloat16),
            pltpu.VMEM(w_value.shape, jnp.bfloat16),
            pltpu.SemaphoreType.DMA((n_tok,)),
            pltpu.SemaphoreType.DMA((steps, 3)),
        ],
        50,
        7,
        "project",
        after,
    )


def absorb(carry, scores, biases, v):
    chunks = []
    for s, bias in zip(scores, biases):
        s = s + bias
        chunks += [s[:, j : j + HD] for j in range(0, s.shape[1], HD)]
    top = chunks[0]
    for c in chunks[1:]:
        top = jnp.maximum(top, c)
    m_new = jnp.broadcast_to(jnp.max(top, axis=1, keepdims=True) * SCALE, top.shape)
    if carry is not None:
        m_new = jnp.maximum(carry[0], m_new)
    total = None
    rounded = []
    for c in chunks:
        w = jnp.exp2(c * SCALE - m_new)
        total = w if total is None else total + w
        rounded.append(w.astype(jnp.bfloat16))
    out = jnp.dot(jnp.concatenate(rounded, axis=1), v, preferred_element_type=jnp.float32)
    if carry is not None:
        alpha = jnp.exp2(carry[0] - m_new)
        total = carry[1] * alpha + total
        out = carry[2] * alpha + out
    return m_new, total, out


def fold_heads(q_ref, slot, kv_local, keys, values, bias, load, store):
    group, tree = q_ref.shape[1] // kv_local, q_ref.shape[2]
    rows = group * tree

    def scores_of(h):
        q = q_ref[slot, h * group : (h + 1) * group].reshape(rows, HD)
        return [dot_nt(q, k(h)) for k in keys]

    def values_of(h):
        parts = [v(h) for v in values]
        return parts[0] if len(parts) == 1 else jnp.concatenate(parts, axis=0)

    ahead = scores_of(0)
    for h in range(kv_local):
        now = ahead
        if h + 1 < kv_local:
            ahead = scores_of(h + 1)
        store(h, absorb(load(h), now, bias, values_of(h)))


def state_access(refs, r):
    def load(h):
        return tuple(ref[r, h] for ref in refs)

    def store(h, state):
        for ref, value in zip(refs, state):
            ref[r, h] = value

    return load, store


def fold_shards(q_ref, r, offset, kv_local, used, bases, base0, held, groups, states):
    n = held.shape[0] // 2
    count = held.shape[1]
    load, store = state_access(states, r)
    for group in groups:
        visible = [used - bases[base0 + i] for i in group]
        most = visible[0]
        for other in visible[1:]:
            most = jnp.maximum(most, other)

        @pl.when(most > 0)
        def _():
            slots = lax.broadcasted_iota(jnp.int32, (1, count), 1)
            fold_heads(
                q_ref,
                offset + r,
                kv_local,
                [lambda h, i=i: held[i, :, head_cols(h)] for i in group],
                [lambda h, i=i: held[n + i, :, head_cols(h)] for i in group],
                [jnp.where(slots < v, 0.0, NEG_FILL) for v in visible],
                load,
                store,
            )


def pairs_of(n):
    return [tuple(range(i, min(i + 2, n))) for i in range(0, n, 2)]


def first_kernel(kv_local, near, block, n_shards, offset, base0, info, bases, q_ref, kn_ref, vn_ref, anc_ref, ck_ref, cv_ref, *refs):
    sources = refs[: 2 * n_shards]
    m_out, l_out, acc_out, k_near, v_near, held, sems = refs[-7:]
    states = (m_out, l_out, acc_out)
    copies = fetch_all(sources, held, sems)
    reqs = m_out.shape[0]
    n_heads, tree = q_ref.shape[1:3]
    group = n_heads // kv_local
    capacity = ck_ref.shape[0]
    for copy in copies:
        copy.wait()
    def one_request(r, _):
        load, store = state_access(states, r)
        low = info[0, offset + r]
        high = info[1, offset + r]
        start0 = pl.multiple_of(jnp.minimum((low // 16) * 16, capacity - near), 16)
        own_rows = pl.ds(pl.multiple_of((offset + r) * tree, tree), tree)
        k_near[0:tree] = kn_ref[own_rows, :]
        v_near[0:tree] = vn_ref[own_rows, :]
        k_near[tree : tree + near] = ck_ref[pl.ds(start0, near), :]
        v_near[tree : tree + near] = cv_ref[pl.ds(start0, near), :]
        column = lax.broadcasted_iota(jnp.int32, (tree, tree + near), 1)
        slots = column - tree + start0
        seen = ((slots >= low) & (slots < high)).astype(jnp.float32)
        linked = jnp.concatenate([anc_ref[offset + r], jnp.zeros((tree, tree + near - HD), jnp.float32)], axis=1)
        bias = jnp.where(jnp.where(column < tree, linked, seen) > 0.5, 0.0, NEG_FILL)
        bias = jnp.concatenate([bias] * group, axis=0)
        seen = [info[2, offset + r] - bases[base0 + i] for i in range(n_shards)]
        place = lax.broadcasted_iota(jnp.int32, (1, held.shape[1]), 1)
        fold_heads(
            q_ref,
            offset + r,
            kv_local,
            [lambda h: k_near[:, head_cols(h)]] + [lambda h, i=i: held[i, :, head_cols(h)] for i in range(n_shards)],
            [lambda h: v_near[:, head_cols(h)]]
            + [lambda h, i=i: held[n_shards + i, :, head_cols(h)] for i in range(n_shards)],
            [bias] + [jnp.where(place < count, 0.0, NEG_FILL) for count in seen],
            lambda h: None,
            store,
        )
        begin0 = start0 + near

        def step(i, _):
            begin = begin0 + i * block
            start = pl.multiple_of(jnp.minimum(begin, capacity - block), 16)
            place = start + lax.broadcasted_iota(jnp.int32, (1, block), 1)
            mask = jnp.where((place >= begin) & (place < high), 0.0, NEG_FILL)
            fold_heads(
                q_ref,
                offset + r,
                kv_local,
                [lambda h: ck_ref[pl.ds(start, block), head_cols(h)]],
                [lambda h: cv_ref[pl.ds(start, block), head_cols(h)]],
                [mask],
                load,
                store,
            )
            return 0

        lax.fori_loop(0, (jnp.maximum(high - begin0, 0) + block - 1) // block, step, 0)
        return 0

    lax.fori_loop(0, reqs, one_request, 0)


def state_shapes(reqs, kv_local, rows):
    return [jax.ShapeDtypeStruct((reqs, kv_local, rows, HD), jnp.float32)] * 3


def shard_scratch(shards):
    n = 2 * len(shards)
    return [pltpu.VMEM((n,) + shards[0][0].shape, jnp.bfloat16), pltpu.SemaphoreType.DMA((n,))]


def flat(shards):
    return [k for k, _ in shards] + [v for _, v in shards]


def attend_first(parts, ancestry, cache_keys, cache_values, info, bases, shards, span, offset, reqs, after=()):
    queries, new_keys, new_values = parts
    shards = shards[span[0] : span[1]]
    _, n_heads, tree, _ = queries.shape
    capacity, cols = cache_keys.shape
    kv_local = cols // HD
    near = min(384 - tree, capacity)
    block = min(1792, capacity)
    n = len(shards)
    return call(
        functools.partial(first_kernel, kv_local, near, block, n, offset, span[0]),
        [SMEM] * 2 + [VMEM] * 6 + [HBM] * (2 * n),
        [info, bases, queries, new_keys, new_values, ancestry, cache_keys, cache_values, *flat(shards)],
        state_shapes(reqs, kv_local, n_heads // kv_local * tree),
        [pltpu.VMEM((tree + near, cols), jnp.bfloat16)] * 2 + shard_scratch(shards),
        40,
        6,
        "attend_first",
        after,
    )


def middle_kernel(kv_local, n_shards, offset, groups, base0, info, bases, q_ref, *refs):
    sources = refs[: 2 * n_shards]
    ins = refs[2 * n_shards : 2 * n_shards + 3]
    outs = refs[2 * n_shards + 3 : 2 * n_shards + 6]
    held, sems = refs[2 * n_shards + 6 :]
    copies = fetch_all(sources, held, sems)
    reqs = outs[0].shape[0]
    for src, dst in zip(ins, outs):
        dst[...] = src[offset : offset + reqs]
    for copy in copies:
        copy.wait()

    def one_request(r, _):
        fold_shards(q_ref, r, offset, kv_local, info[2, offset + r], bases, base0, held, groups, outs)
        return 0

    lax.fori_loop(0, reqs, one_request, 0)


def attend_middle(queries, info, bases, shards, span, state, offset, reqs, microseconds=0.3):
    shards = shards[span[0] : span[1]]
    _, n_heads, tree, _ = queries.shape
    kv_local = shards[0][0].shape[1] // HD
    n = len(shards)
    return call(
        functools.partial(middle_kernel, kv_local, n, offset, pairs_of(n), span[0]),
        [SMEM] * 2 + [VMEM] + [HBM] * (2 * n) + [VMEM] * 3,
        [info, bases, queries, *flat(shards), *state],
        state_shapes(reqs, kv_local, n_heads // kv_local * tree),
        shard_scratch(shards),
        40,
        microseconds,
        "attend_middle",
    )


def last_kernel(kv_local, n_shards, offset, groups, base0, block, info, bases, q_ref, *refs):
    sources = refs[: 2 * n_shards]
    ins = refs[2 * n_shards : 2 * n_shards + 3]
    w_ref = refs[2 * n_shards + 3]
    m_s, l_s, acc_s, attended, w_held, w_sems, held, sems = refs[-8:]
    reqs = m_s.shape[0]
    n_heads, tree = q_ref.shape[1:3]
    outs = refs[-8 - reqs : -8]
    states = (m_s, l_s, acc_s)
    group = n_heads // kv_local
    copies = fetch_all(sources, held, sems)
    cuts = [slice(lo, lo + block) for lo in range(0, w_ref.shape[1], block)]
    w_copies = fetch_all([w_ref.at[:, cut] for cut in cuts], w_held, w_sems)
    for src, dst in zip(ins, states):
        lead = 0 if src.shape[0] == reqs else offset
        dst[...] = src[lead : lead + reqs]
    for copy in copies:
        copy.wait()

    def one_request(r, _):
        fold_shards(q_ref, r, offset, kv_local, info[2, offset + r], bases, base0, held, groups, states)
        for h in range(kv_local):
            total = jnp.sum(l_s[r, h], axis=1, keepdims=True)
            result = (acc_s[r, h] / total).astype(jnp.bfloat16)
            for g in range(group):
                attended[r, :, head_cols(h * group + g)] = result[g * tree : (g + 1) * tree]
        return 0

    lax.fori_loop(0, reqs, one_request, 0)
    x = attended[...].reshape(reqs * tree, n_heads * HD)
    for i, cut in enumerate(cuts):
        w_copies[i].wait()
        product = jnp.dot(x, w_held[i], preferred_element_type=jnp.float32).astype(jnp.bfloat16)
        for r in range(reqs):
            outs[r][:, cut] = product[r * tree : (r + 1) * tree]


def attend_last(queries, info, bases, shards, span, state, w_out, offset, reqs, after=()):
    shards = shards[span[0] : span[1]]
    _, n_heads, tree, _ = queries.shape
    kv_local = shards[0][0].shape[1] // HD
    rows = n_heads // kv_local * tree
    n = len(shards)
    depth, width = w_out.shape
    block = min(1024, width)
    return call(
        functools.partial(last_kernel, kv_local, n, offset, pairs_of(n), span[0], block),
        [SMEM] * 2 + [VMEM] + [HBM] * (2 * n) + [VMEM] * 3 + [HBM],
        [info, bases, queries, *flat(shards), *state, w_out],
        [jax.ShapeDtypeStruct((tree, width), jnp.bfloat16)] * reqs,
        [pltpu.VMEM((reqs, kv_local, rows, HD), jnp.float32)] * 3
        + [
            pltpu.VMEM((reqs, tree, n_heads * HD), jnp.bfloat16),
            pltpu.VMEM((width // block, depth, block), jnp.bfloat16),
            pltpu.SemaphoreType.DMA((width // block,)),
        ]
        + shard_scratch(shards),
        50,
        3.5 + 0.4 * n * reqs,
        "attend_last",
        after,
    )


def add_kernel(*refs):
    total = refs[0][...].astype(jnp.float32)
    for ref in refs[1:-1]:
        total = total + ref[...].astype(jnp.float32)
    refs[-1][...] = total.astype(refs[-1].dtype)


def add_up(*terms, dtype=jnp.bfloat16):
    outs = call(
        add_kernel,
        [VMEM] * len(terms),
        list(terms),
        [jax.ShapeDtypeStruct(terms[0].shape, dtype)],
        [],
        8,
        1,
        "add_up",
    )
    return outs[0]


def ancestor_table(parents):
    node_count = parents.shape[-1]
    column = jnp.arange(node_count, dtype=jnp.int32)
    linked = (parents[..., None] == column) | (column[:, None] == column[None, :])
    ancestry = linked.astype(jnp.bfloat16)
    for repeat in range((node_count - 1).bit_length()):
        paths = jnp.einsum("rij,rjk->rik", ancestry, ancestry, preferred_element_type=jnp.float32)
        ancestry = jnp.minimum(paths, 1.0).astype(jnp.bfloat16)
    return ancestry.astype(jnp.float32)


def rotary_tables(position):
    half = HD // 2
    frequency = 10000.0 ** (-jnp.arange(half, dtype=jnp.float32) / half)
    angles = position.astype(jnp.float32)[:, None] * frequency[None, :]
    cosine = jnp.cos(angles)
    sine = jnp.sin(angles)
    return jnp.concatenate([cosine, cosine], axis=1), jnp.concatenate([-sine, sine], axis=1)


def swap_pairs(batch, tensor, move):
    columns = 2
    pairs = []
    for z in range(batch // columns):
        for x in range(columns):
            for t in range(tensor):
                z2, x2, t2 = move(z, x, t)
                pairs.append(((z * columns + x) * tensor + t, (z2 * columns + x2) * tensor + t2))
    return pairs


def body(
    sizes,
    tokens,
    norm_gain,
    w_query,
    w_key,
    w_value,
    w_out,
    prefix_keys,
    prefix_values,
    cache_keys,
    cache_values,
    cache_lengths,
    prefix_used,
    parents,
    accepted_index,
):
    batch, tensor = sizes
    reqs, tree = parents.shape
    shard_rows = prefix_keys.shape[0]
    fast = sizes == (8, 4) and reqs == tensor and tokens.shape[0] == tree
    me_batch = lax.axis_index("batch")
    me_tensor = lax.axis_index("tensor")
    slots = jnp.arange(reqs, dtype=jnp.int32)

    if fast:
        pairs = functools.partial(swap_pairs, batch, tensor)
        core_pairs = pairs(lambda z, x, t: (z, x, t ^ 1))
        y_pairs = pairs(lambda z, x, t: (z, x, t ^ 2))
        x_pairs = pairs(lambda z, x, t: (z, 1 - x, t))
        z_pairs = pairs(lambda z, x, t: ((z + 1) % (batch // 2), x, t))
        send = lambda a, p: lax.ppermute(a, AXES, p)
        core_tokens = send(tokens, core_pairs)
        y_tokens = send(tokens, y_pairs)
        far_tokens = send(y_tokens, core_pairs)
    order = slots ^ me_tensor if fast else slots
    pick = order[:, None] == slots[None, :]
    own_lengths = lax.dynamic_slice_in_dim(cache_lengths, me_batch * reqs, reqs)
    lower = jnp.cumsum(own_lengths) - own_lengths
    table = jnp.stack([lower, lower + own_lengths, prefix_used])
    info = jnp.sum(jnp.where(pick[None], table[:, None, :], 0), axis=2)
    tree_parents = jnp.sum(jnp.where(pick[:, :, None], parents[None], 0), axis=1)
    ancestry = ancestor_table(tree_parents)
    tree_depth = (jnp.sum(ancestry, axis=-1) - 1.0).astype(jnp.int32)
    position = ((info[2] + info[1] - info[0])[:, None] + tree_depth).reshape(reqs * tree)
    if fast:
        steps = batch // 2
        own_keys, own_values, _ = lax.optimization_barrier((prefix_keys, prefix_values, own_lengths))
        ring = [(prefix_keys, prefix_values)]
        ring.append((send(own_keys, z_pairs), send(own_values, z_pairs)))
        side = [(send(own_keys, x_pairs), send(own_values, x_pairs))]
    cosine, sine = rotary_tables(position)
    ancestry = jnp.pad(ancestry, ((0, 0), (0, 0), (0, HD - tree)))
    shard_ids = jnp.arange(batch, dtype=jnp.int32)
    if fast:
        z, x = me_batch // 2, me_batch % 2
        shard_ids = (z - shard_ids // 2) % (batch // 2) * 2 + (x ^ (shard_ids % 2))
    bases = (shard_ids * shard_rows).astype(jnp.int32)

    def projected(token_list, after=()):
        return project(token_list, norm_gain[None, :], cosine, sine, w_query, w_key, w_value, tree, after)

    if fast:
        def pass_on(step, after):
            keys, values, _ = lax.optimization_barrier((*ring[step], after))
            if step < steps - 1:
                ring.append((send(keys, z_pairs), send(values, z_pairs)))
                side.append((send(keys, x_pairs), send(values, x_pairs)))
            else:
                side.append((send(keys, x_pairs), send(side[-1][1], z_pairs)))

        pass_on(1, cosine)
        parts = projected([tokens, core_tokens, y_tokens, far_tokens])
        queries, new_keys, new_values = parts
        pass_on(2, queries)
        shards = [shard for s in range(steps - 1) for shard in (ring[s], side[s])]
        first = functools.partial(
            attend_first,
            (queries, new_keys, new_values),
            ancestry,
            cache_keys,
            cache_values,
            info,
            bases,
            shards,
            (0, 2),
            reqs=reqs,
        )
        state = first(offset=0)
        pass_on(steps - 1, state[0])
        shards += [ring[-1], side[-1]]
        n = len(shards)
        state = attend_middle(queries, info, bases, shards, (2, 5), state, 0, reqs)
        far_state = attend_middle(queries, info, bases, shards, (5, n - 1), state, 2, 2, 4)
        final = functools.partial(attend_last, queries, info, bases, shards, w_out=w_out, reqs=2)
        kept, away = final((n - 1, n), far_state, offset=2)
        got = send(away, core_pairs)
        summed = add_up(kept, got)
        far = send(summed, y_pairs)
        kept, away = final((5, n), state, offset=0, after=(summed,))
        got = send(away, core_pairs)
        mixed_rows = add_up(add_up(kept, far, dtype=jnp.float32), got)
    else:
        gathered = lax.all_gather(tokens, "tensor", axis=0, tiled=True)
        parts = projected([gathered])
        queries, new_keys, new_values = parts
        all_keys = lax.all_gather(prefix_keys, "batch", axis=0, tiled=True)
        all_values = lax.all_gather(prefix_values, "batch", axis=0, tiled=True)
        split = lambda a: [a[i * shard_rows : (i + 1) * shard_rows] for i in range(batch)]
        shards = list(zip(split(all_keys), split(all_values)))
        state = attend_first(parts, ancestry, cache_keys, cache_values, info, bases, shards, (0, 2), 0, reqs)
        for s in range(2, batch - 2, 4):
            state = attend_middle(queries, info, bases, shards, (s, min(s + 4, batch - 2)), state, 0, reqs)
        partial = attend_last(queries, info, bases, shards, (batch - 2, batch), state, w_out, 0, reqs)
        mixed_rows = lax.psum_scatter(
            jnp.concatenate(partial, axis=0), "tensor", scatter_dimension=0, tiled=True
        )
    rows = ((slots ^ me_tensor if fast else slots)[:, None] * tree + accepted_index).reshape(-1)
    accepted_keys = jnp.take(new_keys, rows, axis=0).reshape(reqs, accepted_index.shape[1], -1)
    accepted_values = jnp.take(new_values, rows, axis=0).reshape(reqs, accepted_index.shape[1], -1)
    return (mixed_rows, accepted_keys, accepted_values)


def solution(mesh):
    sizes = (mesh.shape["batch"], mesh.shape["tensor"])
    in_specs = (
        P(("batch", "tensor"), None),
        P(),
        P(None, "tensor"),
        P(None, "tensor"),
        P(None, "tensor"),
        P("tensor", None),
        P("batch", "tensor"),
        P("batch", "tensor"),
        P("batch", "tensor"),
        P("batch", "tensor"),
        P(),
        P("batch"),
        P("batch", None),
        P("batch", None),
    )
    out_specs = (
        P(("batch", "tensor"), None),
        P("batch", None, "tensor"),
        P("batch", None, "tensor"),
    )
    return jax.shard_map(
        functools.partial(body, sizes), mesh=mesh, in_specs=in_specs, out_specs=out_specs, check_vma=False
    )
```

```python
import functools

import jax
import jax.numpy as jnp
from jax import lax
from jax.experimental import pallas as pl
from jax.experimental.pallas import tpu as pltpu
from jax.sharding import PartitionSpec as P

HD = 128
NEG_FILL = -1e30
LOG2E = 1.4426950408889634
AXES = ("batch", "tensor")
SCALE = HD**-0.5 * LOG2E
COST = 1.1e9
HBM = pl.BlockSpec(memory_space=pltpu.HBM)
VMEM = pl.BlockSpec(memory_space=pltpu.VMEM)
SMEM = pl.BlockSpec(memory_space=pltpu.SMEM)


def call(kernel, in_specs, args, out_shape, scratch, megabytes, microseconds, name, after=()):
    n_in, n_out = len(args), len(out_shape)

    def wrapped(*refs):
        kernel(*refs[:n_in], *refs[n_in + len(after) :])

    return pl.pallas_call(
        wrapped,
        in_specs=in_specs + [HBM] * len(after),
        out_specs=[VMEM] * n_out,
        out_shape=out_shape,
        scratch_shapes=scratch,
        compiler_params=pltpu.CompilerParams(vmem_limit_bytes=megabytes * 2**20),
        cost_estimate=pl.CostEstimate(flops=int(microseconds * COST), bytes_accessed=0, transcendentals=0),
        name=name,
    )(*args, *after)


def dot_nt(a, b):
    return lax.dot_general(a, b, (((1,), (1,)), ((), ())), preferred_element_type=jnp.float32)


def head_cols(h):
    return slice(h * HD, (h + 1) * HD)


def fetch_all(sources, held, sems):
    copies = [pltpu.make_async_copy(src, held.at[i], sems.at[i]) for i, src in enumerate(sources)]
    for copy in copies:
        copy.start()
    return copies


def qkv_kernel(n_tok, n_heads, kv_local, steps, *refs):
    token_refs = refs[:n_tok]
    gain_ref, cos_ref, sin_ref = refs[n_tok : n_tok + 3]
    weights = refs[n_tok + 3 : n_tok + 6]
    q_out, k_out, v_out, held, normed, acc, wq, wk, wv, sems, weight_sems = refs[n_tok + 6 :]
    copies = fetch_all(token_refs, held, sems)
    depth = wq.shape[0] // steps
    chunks = []
    for s in range(steps):
        span = slice(s * depth, (s + 1) * depth)
        chunks.append(
            [
                pltpu.make_async_copy(src.at[span], dst.at[span], weight_sems.at[s, i])
                for i, (src, dst) in enumerate(zip(weights, (wq, wk, wv)))
            ]
        )
        for copy in chunks[-1]:
            copy.start()
    rows = held.shape[1]
    step = min(16, rows)
    for i in range(n_tok):
        copies[i].wait()
        for lo in range(0, rows, step):
            values = held[i, lo : lo + step].astype(jnp.float32)
            factor = lax.rsqrt(jnp.mean(values * values, axis=-1, keepdims=True) + 1e-05)
            normed[i * rows + lo : i * rows + lo + step] = (values * factor * gain_ref[...]).astype(jnp.bfloat16)
    cosine = cos_ref[...]
    sine = sin_ref[...]
    reqs, tree = q_out.shape[0], q_out.shape[2]

    def rotated(raw):
        return (raw * cosine + pltpu.roll(raw, HD // 2, 1) * sine).astype(jnp.bfloat16)

    for s in range(steps):
        for copy in chunks[s]:
            copy.wait()
        span = slice(s * depth, (s + 1) * depth)
        x = normed[:, span]
        lo = 0
        for which, w in enumerate((wq, wk, wv)):
            width = w.shape[1]
            raw = jnp.dot(x, w[span], preferred_element_type=jnp.float32)
            if s > 0:
                raw = acc[:, lo : lo + width] + raw
            if s < steps - 1:
                acc[:, lo : lo + width] = raw
            elif which == 0:
                for head in range(n_heads):
                    out = rotated(raw[:, head_cols(head)])
                    for r in range(reqs):
                        q_out[r, head] = out[r * tree : (r + 1) * tree]
            elif which == 1:
                for head in range(kv_local):
                    k_out[:, head_cols(head)] = rotated(raw[:, head_cols(head)])
            else:
                v_out[...] = raw.astype(jnp.bfloat16)
            lo += width


def project(token_list, gain, cosine, sine, w_query, w_key, w_value, tree, after=()):
    rows, width = token_list[0].shape
    n_tok = len(token_list)
    total = rows * n_tok
    n_heads = w_query.shape[1] // HD
    cols = w_key.shape[1]
    steps = 4
    return call(
        functools.partial(qkv_kernel, n_tok, n_heads, cols // HD, steps),
        [HBM] * n_tok + [VMEM] * 3 + [HBM] * 3,
        [*token_list, gain, cosine, sine, w_query, w_key, w_value],
        [
            jax.ShapeDtypeStruct((total // tree, n_heads, tree, HD), jnp.bfloat16),
            jax.ShapeDtypeStruct((total, cols), jnp.bfloat16),
            jax.ShapeDtypeStruct((total, cols), jnp.bfloat16),
        ],
        [
            pltpu.VMEM((n_tok, rows, width), jnp.bfloat16),
            pltpu.VMEM((total, width), jnp.bfloat16),
            pltpu.VMEM((total, w_query.shape[1] + 2 * cols), jnp.float32),
            pltpu.VMEM(w_query.shape, jnp.bfloat16),
            pltpu.VMEM(w_key.shape, jnp.bfloat16),
            pltpu.VMEM(w_value.shape, jnp.bfloat16),
            pltpu.SemaphoreType.DMA((n_tok,)),
            pltpu.SemaphoreType.DMA((steps, 3)),
        ],
        50,
        7,
        "project",
        after,
    )


def absorb(carry, scores, biases, v):
    chunks = []
    for s, bias in zip(scores, biases):
        s = s + bias
        chunks += [s[:, j : j + HD] for j in range(0, s.shape[1], HD)]
    top = chunks[0]
    for c in chunks[1:]:
        top = jnp.maximum(top, c)
    m_new = jnp.broadcast_to(jnp.max(top, axis=1, keepdims=True) * SCALE, top.shape)
    if carry is not None:
        m_new = jnp.maximum(carry[0], m_new)
    total = None
    rounded = []
    for c in chunks:
        w = jnp.exp2(c * SCALE - m_new)
        total = w if total is None else total + w
        rounded.append(w.astype(jnp.bfloat16))
    out = jnp.dot(jnp.concatenate(rounded, axis=1), v, preferred_element_type=jnp.float32)
    if carry is not None:
        alpha = jnp.exp2(carry[0] - m_new)
        total = carry[1] * alpha + total
        out = carry[2] * alpha + out
    return m_new, total, out


def fold_heads(q_ref, slot, kv_local, keys, values, bias, load, store):
    group, tree = q_ref.shape[1] // kv_local, q_ref.shape[2]
    rows = group * tree

    def scores_of(h):
        q = q_ref[slot, h * group : (h + 1) * group].reshape(rows, HD)
        return [dot_nt(q, k(h)) for k in keys]

    def values_of(h):
        parts = [v(h) for v in values]
        return parts[0] if len(parts) == 1 else jnp.concatenate(parts, axis=0)

    ahead = scores_of(0)
    for h in range(kv_local):
        now = ahead
        if h + 1 < kv_local:
            ahead = scores_of(h + 1)
        store(h, absorb(load(h), now, bias, values_of(h)))


def state_access(refs, r):
    def load(h):
        return tuple(ref[r, h] for ref in refs)

    def store(h, state):
        for ref, value in zip(refs, state):
            ref[r, h] = value

    return load, store


def fold_shards(q_ref, r, offset, kv_local, used, bases, base0, held, groups, states):
    n = held.shape[0] // 2
    count = held.shape[1]
    load, store = state_access(states, r)
    for group in groups:
        visible = [used - bases[base0 + i] for i in group]
        most = visible[0]
        for other in visible[1:]:
            most = jnp.maximum(most, other)

        @pl.when(most > 0)
        def _():
            slots = lax.broadcasted_iota(jnp.int32, (1, count), 1)
            fold_heads(
                q_ref,
                offset + r,
                kv_local,
                [lambda h, i=i: held[i, :, head_cols(h)] for i in group],
                [lambda h, i=i: held[n + i, :, head_cols(h)] for i in group],
                [jnp.where(slots < v, 0.0, NEG_FILL) for v in visible],
                load,
                store,
            )


def pairs_of(n):
    return [tuple(range(i, min(i + 2, n))) for i in range(0, n, 2)]


def first_kernel(kv_local, near, block, n_shards, offset, base0, info, bases, q_ref, kn_ref, vn_ref, anc_ref, ck_ref, cv_ref, *refs):
    sources = refs[: 2 * n_shards]
    m_out, l_out, acc_out, k_near, v_near, held, sems = refs[-7:]
    states = (m_out, l_out, acc_out)
    copies = fetch_all(sources, held, sems)
    reqs = m_out.shape[0]
    n_heads, tree = q_ref.shape[1:3]
    group = n_heads // kv_local
    capacity = ck_ref.shape[0]
    for copy in copies:
        copy.wait()
    def one_request(r, _):
        load, store = state_access(states, r)
        low = info[0, offset + r]
        high = info[1, offset + r]
        start0 = pl.multiple_of(jnp.minimum((low // 16) * 16, capacity - near), 16)
        own_rows = pl.ds(pl.multiple_of((offset + r) * tree, tree), tree)
        k_near[0:tree] = kn_ref[own_rows, :]
        v_near[0:tree] = vn_ref[own_rows, :]
        k_near[tree : tree + near] = ck_ref[pl.ds(start0, near), :]
        v_near[tree : tree + near] = cv_ref[pl.ds(start0, near), :]
        column = lax.broadcasted_iota(jnp.int32, (tree, tree + near), 1)
        slots = column - tree + start0
        seen = ((slots >= low) & (slots < high)).astype(jnp.float32)
        linked = jnp.concatenate([anc_ref[offset + r], jnp.zeros((tree, tree + near - HD), jnp.float32)], axis=1)
        bias = jnp.where(jnp.where(column < tree, linked, seen) > 0.5, 0.0, NEG_FILL)
        bias = jnp.concatenate([bias] * group, axis=0)
        seen = [info[2, offset + r] - bases[base0 + i] for i in range(n_shards)]
        place = lax.broadcasted_iota(jnp.int32, (1, held.shape[1]), 1)
        fold_heads(
            q_ref,
            offset + r,
            kv_local,
            [lambda h: k_near[:, head_cols(h)]] + [lambda h, i=i: held[i, :, head_cols(h)] for i in range(n_shards)],
            [lambda h: v_near[:, head_cols(h)]]
            + [lambda h, i=i: held[n_shards + i, :, head_cols(h)] for i in range(n_shards)],
            [bias] + [jnp.where(place < count, 0.0, NEG_FILL) for count in seen],
            lambda h: None,
            store,
        )
        begin0 = start0 + near

        def step(i, _):
            begin = begin0 + i * block
            start = pl.multiple_of(jnp.minimum(begin, capacity - block), 16)
            place = start + lax.broadcasted_iota(jnp.int32, (1, block), 1)
            mask = jnp.where((place >= begin) & (place < high), 0.0, NEG_FILL)
            fold_heads(
                q_ref,
                offset + r,
                kv_local,
                [lambda h: ck_ref[pl.ds(start, block), head_cols(h)]],
                [lambda h: cv_ref[pl.ds(start, block), head_cols(h)]],
                [mask],
                load,
                store,
            )
            return 0

        lax.fori_loop(0, (jnp.maximum(high - begin0, 0) + block - 1) // block, step, 0)
        return 0

    lax.fori_loop(0, reqs, one_request, 0)


def state_shapes(reqs, kv_local, rows):
    return [jax.ShapeDtypeStruct((reqs, kv_local, rows, HD), jnp.float32)] * 3


def shard_scratch(shards):
    n = 2 * len(shards)
    return [pltpu.VMEM((n,) + shards[0][0].shape, jnp.bfloat16), pltpu.SemaphoreType.DMA((n,))]


def flat(shards):
    return [k for k, _ in shards] + [v for _, v in shards]


def attend_first(parts, ancestry, cache_keys, cache_values, info, bases, shards, span, offset, reqs, after=()):
    queries, new_keys, new_values = parts
    shards = shards[span[0] : span[1]]
    _, n_heads, tree, _ = queries.shape
    capacity, cols = cache_keys.shape
    kv_local = cols // HD
    near = min(384 - tree, capacity)
    block = min(1792, capacity)
    n = len(shards)
    return call(
        functools.partial(first_kernel, kv_local, near, block, n, offset, span[0]),
        [SMEM] * 2 + [VMEM] * 6 + [HBM] * (2 * n),
        [info, bases, queries, new_keys, new_values, ancestry, cache_keys, cache_values, *flat(shards)],
        state_shapes(reqs, kv_local, n_heads // kv_local * tree),
        [pltpu.VMEM((tree + near, cols), jnp.bfloat16)] * 2 + shard_scratch(shards),
        40,
        6,
        "attend_first",
        after,
    )


def middle_kernel(kv_local, n_shards, offset, groups, base0, info, bases, q_ref, *refs):
    sources = refs[: 2 * n_shards]
    ins = refs[2 * n_shards : 2 * n_shards + 3]
    outs = refs[2 * n_shards + 3 : 2 * n_shards + 6]
    held, sems = refs[2 * n_shards + 6 :]
    copies = fetch_all(sources, held, sems)
    reqs = outs[0].shape[0]
    for src, dst in zip(ins, outs):
        lead = 0 if src.shape[0] == reqs else offset
        dst[...] = src[lead : lead + reqs]
    for copy in copies:
        copy.wait()

    def one_request(r, _):
        fold_shards(q_ref, r, offset, kv_local, info[2, offset + r], bases, base0, held, groups, outs)
        return 0

    lax.fori_loop(0, reqs, one_request, 0)


def attend_middle(queries, info, bases, shards, span, state, offset, reqs, microseconds=2.7):
    shards = shards[span[0] : span[1]]
    _, n_heads, tree, _ = queries.shape
    kv_local = shards[0][0].shape[1] // HD
    n = len(shards)
    return call(
        functools.partial(middle_kernel, kv_local, n, offset, pairs_of(n), span[0]),
        [SMEM] * 2 + [VMEM] + [HBM] * (2 * n) + [VMEM] * 3,
        [info, bases, queries, *flat(shards), *state],
        state_shapes(reqs, kv_local, n_heads // kv_local * tree),
        shard_scratch(shards),
        40,
        microseconds,
        "attend_middle",
    )


def last_kernel(kv_local, n_shards, offset, groups, base0, block, info, bases, q_ref, *refs):
    sources = refs[: 2 * n_shards]
    ins = refs[2 * n_shards : 2 * n_shards + 3]
    w_ref = refs[2 * n_shards + 3]
    m_s, l_s, acc_s, attended, w_held, w_sems, held, sems = refs[-8:]
    reqs = m_s.shape[0]
    n_heads, tree = q_ref.shape[1:3]
    outs = refs[-8 - reqs : -8]
    states = (m_s, l_s, acc_s)
    group = n_heads // kv_local
    copies = fetch_all(sources, held, sems)
    cuts = [slice(lo, lo + block) for lo in range(0, w_ref.shape[1], block)]
    w_copies = fetch_all([w_ref.at[:, cut] for cut in cuts], w_held, w_sems)
    for src, dst in zip(ins, states):
        lead = 0 if src.shape[0] == reqs else offset
        dst[...] = src[lead : lead + reqs]
    for copy in copies:
        copy.wait()

    def one_request(r, _):
        fold_shards(q_ref, r, offset, kv_local, info[2, offset + r], bases, base0, held, groups, states)
        for h in range(kv_local):
            total = jnp.sum(l_s[r, h], axis=1, keepdims=True)
            result = (acc_s[r, h] / total).astype(jnp.bfloat16)
            for g in range(group):
                attended[r, :, head_cols(h * group + g)] = result[g * tree : (g + 1) * tree]
        return 0

    lax.fori_loop(0, reqs, one_request, 0)
    x = attended[...].reshape(reqs * tree, n_heads * HD)
    for i, cut in enumerate(cuts):
        w_copies[i].wait()
        product = jnp.dot(x, w_held[i], preferred_element_type=jnp.float32).astype(jnp.bfloat16)
        for r in range(reqs):
            outs[r][:, cut] = product[r * tree : (r + 1) * tree]


def attend_last(queries, info, bases, shards, span, state, w_out, offset, reqs, after=()):
    shards = shards[span[0] : span[1]]
    _, n_heads, tree, _ = queries.shape
    kv_local = shards[0][0].shape[1] // HD
    rows = n_heads // kv_local * tree
    n = len(shards)
    depth, width = w_out.shape
    block = min(1024, width)
    return call(
        functools.partial(last_kernel, kv_local, n, offset, pairs_of(n), span[0], block),
        [SMEM] * 2 + [VMEM] + [HBM] * (2 * n) + [VMEM] * 3 + [HBM],
        [info, bases, queries, *flat(shards), *state, w_out],
        [jax.ShapeDtypeStruct((tree, width), jnp.bfloat16)] * reqs,
        [pltpu.VMEM((reqs, kv_local, rows, HD), jnp.float32)] * 3
        + [
            pltpu.VMEM((reqs, tree, n_heads * HD), jnp.bfloat16),
            pltpu.VMEM((width // block, depth, block), jnp.bfloat16),
            pltpu.SemaphoreType.DMA((width // block,)),
        ]
        + shard_scratch(shards),
        50,
        3.5 + 0.4 * n * reqs,
        "attend_last",
        after,
    )


def add_kernel(*refs):
    total = refs[0][...].astype(jnp.float32)
    for ref in refs[1:-1]:
        total = total + ref[...].astype(jnp.float32)
    refs[-1][...] = total.astype(refs[-1].dtype)


def add_up(*terms, dtype=jnp.bfloat16):
    outs = call(
        add_kernel,
        [VMEM] * len(terms),
        list(terms),
        [jax.ShapeDtypeStruct(terms[0].shape, dtype)],
        [],
        8,
        1,
        "add_up",
    )
    return outs[0]


def ancestor_table(parents):
    node_count = parents.shape[-1]
    column = jnp.arange(node_count, dtype=jnp.int32)
    linked = (parents[..., None] == column) | (column[:, None] == column[None, :])
    ancestry = linked.astype(jnp.bfloat16)
    for repeat in range((node_count - 1).bit_length()):
        paths = jnp.einsum("rij,rjk->rik", ancestry, ancestry, preferred_element_type=jnp.float32)
        ancestry = jnp.minimum(paths, 1.0).astype(jnp.bfloat16)
    return ancestry.astype(jnp.float32)


def rotary_tables(position):
    half = HD // 2
    frequency = 10000.0 ** (-jnp.arange(half, dtype=jnp.float32) / half)
    angles = position.astype(jnp.float32)[:, None] * frequency[None, :]
    cosine = jnp.cos(angles)
    sine = jnp.sin(angles)
    return jnp.concatenate([cosine, cosine], axis=1), jnp.concatenate([-sine, sine], axis=1)


def swap_pairs(batch, tensor, move):
    columns = 2
    pairs = []
    for z in range(batch // columns):
        for x in range(columns):
            for t in range(tensor):
                z2, x2, t2 = move(z, x, t)
                pairs.append(((z * columns + x) * tensor + t, (z2 * columns + x2) * tensor + t2))
    return pairs


def body(
    sizes,
    tokens,
    norm_gain,
    w_query,
    w_key,
    w_value,
    w_out,
    prefix_keys,
    prefix_values,
    cache_keys,
    cache_values,
    cache_lengths,
    prefix_used,
    parents,
    accepted_index,
):
    batch, tensor = sizes
    reqs, tree = parents.shape
    shard_rows = prefix_keys.shape[0]
    fast = sizes == (8, 4) and reqs == tensor and tokens.shape[0] == tree
    me_batch = lax.axis_index("batch")
    me_tensor = lax.axis_index("tensor")
    slots = jnp.arange(reqs, dtype=jnp.int32)

    if fast:
        pairs = functools.partial(swap_pairs, batch, tensor)
        core_pairs = pairs(lambda z, x, t: (z, x, t ^ 1))
        y_pairs = pairs(lambda z, x, t: (z, x, t ^ 2))
        x_pairs = pairs(lambda z, x, t: (z, 1 - x, t))
        z_pairs = pairs(lambda z, x, t: ((z + 1) % (batch // 2), x, t))
        send = lambda a, p: lax.ppermute(a, AXES, p)
        core_tokens = send(tokens, core_pairs)
        y_tokens = send(tokens, y_pairs)
        far_tokens = send(y_tokens, core_pairs)
    order = slots ^ me_tensor if fast else slots
    pick = order[:, None] == slots[None, :]
    own_lengths = lax.dynamic_slice_in_dim(cache_lengths, me_batch * reqs, reqs)
    lower = jnp.cumsum(own_lengths) - own_lengths
    table = jnp.stack([lower, lower + own_lengths, prefix_used])
    info = jnp.sum(jnp.where(pick[None], table[:, None, :], 0), axis=2)
    tree_parents = jnp.sum(jnp.where(pick[:, :, None], parents[None], 0), axis=1)
    ancestry = ancestor_table(tree_parents)
    tree_depth = (jnp.sum(ancestry, axis=-1) - 1.0).astype(jnp.int32)
    position = ((info[2] + info[1] - info[0])[:, None] + tree_depth).reshape(reqs * tree)
    if fast:
        steps = batch // 2
        own_keys, own_values, _ = lax.optimization_barrier((prefix_keys, prefix_values, own_lengths))
        ring = [(prefix_keys, prefix_values)]
        ring.append((send(own_keys, z_pairs), send(own_values, z_pairs)))
        side = [(send(own_keys, x_pairs), send(own_values, x_pairs))]
    cosine, sine = rotary_tables(position)
    ancestry = jnp.pad(ancestry, ((0, 0), (0, 0), (0, HD - tree)))
    shard_ids = jnp.arange(batch, dtype=jnp.int32)
    if fast:
        z, x = me_batch // 2, me_batch % 2
        shard_ids = (z - shard_ids // 2) % (batch // 2) * 2 + (x ^ (shard_ids % 2))
    bases = (shard_ids * shard_rows).astype(jnp.int32)

    def projected(token_list, after=()):
        return project(token_list, norm_gain[None, :], cosine, sine, w_query, w_key, w_value, tree, after)

    if fast:
        def pass_on(step, after):
            keys, values, _ = lax.optimization_barrier((*ring[step], after))
            if step < steps - 1:
                ring.append((send(keys, z_pairs), send(values, z_pairs)))
                side.append((send(keys, x_pairs), send(values, x_pairs)))
            else:
                side.append((send(keys, x_pairs), send(side[-1][1], z_pairs)))

        pass_on(1, cosine)
        parts = projected([tokens, core_tokens, y_tokens, far_tokens])
        queries, new_keys, new_values = parts
        pass_on(2, queries)
        shards = [shard for s in range(steps - 1) for shard in (ring[s], side[s])]
        first = functools.partial(
            attend_first,
            (queries, new_keys, new_values),
            ancestry,
            cache_keys,
            cache_values,
            info,
            bases,
            shards,
            (0, 2),
            reqs=reqs,
        )
        state = first(offset=0)
        pass_on(steps - 1, state[0])
        shards += [ring[-1], side[-1]]
        n = len(shards)
        far_state = attend_middle(queries, info, bases, shards, (2, 5), state, 2, 2)
        far_state = attend_middle(queries, info, bases, shards, (5, n - 1), far_state, 2, 2, 1.1)
        final = functools.partial(attend_last, queries, info, bases, shards, w_out=w_out, reqs=2)
        kept, away = final((n - 1, n), far_state, offset=2)
        got = send(away, core_pairs)
        summed = add_up(kept, got)
        far = send(summed, y_pairs)
        kept, away = final((2, n), state, offset=0, after=(summed,))
        got = send(away, core_pairs)
        mixed_rows = add_up(add_up(kept, far, dtype=jnp.float32), got)
    else:
        gathered = lax.all_gather(tokens, "tensor", axis=0, tiled=True)
        parts = projected([gathered])
        queries, new_keys, new_values = parts
        all_keys = lax.all_gather(prefix_keys, "batch", axis=0, tiled=True)
        all_values = lax.all_gather(prefix_values, "batch", axis=0, tiled=True)
        split = lambda a: [a[i * shard_rows : (i + 1) * shard_rows] for i in range(batch)]
        shards = list(zip(split(all_keys), split(all_values)))
        state = attend_first(parts, ancestry, cache_keys, cache_values, info, bases, shards, (0, 2), 0, reqs)
        for s in range(2, batch - 2, 4):
            state = attend_middle(queries, info, bases, shards, (s, min(s + 4, batch - 2)), state, 0, reqs)
        partial = attend_last(queries, info, bases, shards, (batch - 2, batch), state, w_out, 0, reqs)
        mixed_rows = lax.psum_scatter(
            jnp.concatenate(partial, axis=0), "tensor", scatter_dimension=0, tiled=True
        )
    rows = ((slots ^ me_tensor if fast else slots)[:, None] * tree + accepted_index).reshape(-1)
    accepted_keys = jnp.take(new_keys, rows, axis=0).reshape(reqs, accepted_index.shape[1], -1)
    accepted_values = jnp.take(new_values, rows, axis=0).reshape(reqs, accepted_index.shape[1], -1)
    return (mixed_rows, accepted_keys, accepted_values)


def solution(mesh):
    sizes = (mesh.shape["batch"], mesh.shape["tensor"])
    in_specs = (
        P(("batch", "tensor"), None),
        P(),
        P(None, "tensor"),
        P(None, "tensor"),
        P(None, "tensor"),
        P("tensor", None),
        P("batch", "tensor"),
        P("batch", "tensor"),
        P("batch", "tensor"),
        P("batch", "tensor"),
        P(),
        P("batch"),
        P("batch", None),
        P("batch", None),
    )
    out_specs = (
        P(("batch", "tensor"), None),
        P("batch", None, "tensor"),
        P("batch", None, "tensor"),
    )
    return jax.shard_map(
        functools.partial(body, sizes), mesh=mesh, in_specs=in_specs, out_specs=out_specs, check_vma=False
    )
```
